32 devices in a mesh: section: 2 (over core), wide: 4 (over y, x), rep: 4 (over z).
Axes of the slice: x: 2, y: 2, z: 4, core: 2. Of those that a mesh axis runs over, the one named last changes fastest.
Arguments:
- tokens_in: bfloat16 [2, 4096, 1024], P(None, ('rep', 'wide')), may hold values from -6 to 6
- cotangent: bfloat16 [2, 4096, 1024], P(None, ('rep', 'wide')), may hold values from -6 to 6
- segments: int32 [2, 4096], P(None, 'rep'), may hold values from 0 to 15, never falling along the last dimension, each value on 1 to 1024 neighbouring positions
- routes: int32 [2, 2, 4096, 1], P('section', None, ('rep', 'wide')), may hold values from 0 to 3; in each aligned block of 256 rows (0 to 255, 256 to 511, ..., all dimensions but the last counted through in order) at most 64 rows name the same one
- ln1_gain: float32 [2, 1024], P('section'), may hold values from 0.5 to 1.5
- w_qkv: bfloat16 [2, 1024, 3072], P('section', None, 'wide'), may hold values from -0.1875 to 0.1875
- w_out: bfloat16 [2, 1024, 1024], P('section', 'wide'), may hold values from -2 to 2
- ln2_gain: float32 [2, 1024], P('section'), may hold values from 0.5 to 1.5
- w_up: bfloat16 [2, 1024, 4096], P('section', None, 'wide'), may hold values from -0.1875 to 0.1875
- w_down: bfloat16 [2, 4096, 1024], P('section', 'wide'), may hold values from -0.09375 to 0.09375
- centroids: bfloat16 [2, 4, 1024], P('section', 'wide'), may hold values from -0.125 to 0.125
- sub_gains: float32 [2, 4, 2, 1024], P('section', 'wide'), may hold values from 0.5 to 1.5
- expert_up: bfloat16 [2, 4, 2, 1024, 4096], P('section', 'wide', None, None, 'rep'), may hold values from -0.1875 to 0.1875
- expert_down: bfloat16 [2, 4, 2, 4096, 1024], P('section', 'wide', None, 'rep'), may hold values from -0.09375 to 0.09375
Outputs:
- block_out: bfloat16 [2, 4096, 1024], P(None, ('rep', 'wide'), 'section')
- input_grad: float32 [2, 4096, 1024], P(None, ('rep', 'wide'), 'section')
- grad_ln1: float32 [2, 1024], P('section', ('wide', 'rep'))
- grad_w_qkv: float32 [2, 1024, 3072], P('section', 'rep', 'wide')
- grad_w_out: float32 [2, 1024, 1024], P('section', 'wide', 'rep')
- grad_ln2: float32 [2, 1024], P('section', ('wide', 'rep'))
- grad_w_up: float32 [2, 1024, 4096], P('section', 'rep', 'wide')
- grad_w_down: float32 [2, 4096, 1024], P('section', 'wide', 'rep')
- grad_centroids: float32 [2, 4, 1024], P('section', 'wide', 'rep')
- grad_sub_gains: float32 [2, 4, 2, 1024], P('section', 'wide', None, 'rep')
- grad_expert_up: float32 [2, 4, 2, 1024, 4096], P('section', 'wide', None, None, 'rep')
- grad_expert_down: float32 [2, 4, 2, 4096, 1024], P('section', 'wide', None, 'rep')
The draws below stay inside these ranges and needn't reach their ends.
Inputs may be any that keep to these rules, and one draw needn't show every extreme that they name: `routes`: among the 256 tokens of one device (aligned blocks of 256 rows of the flattened array), no expert is named more than 64 times, a bound that some block reaches. `segments`: along each micro-batch's tokens the numbers never fall; a document has at most 1024 tokens.
All inputs are finite; a program needn't handle non-finite values.
Results may differ from the reference program's by a relative error of at most 0.025.
Values may be sent and summed in bfloat16 or wider, within the bound.
No kernel may reach another device: no remote copies, remote signals or barrier semaphores. Data moves between devices by JAX's collectives and lax.ppermute only.
A program may use at most 448 MiB of HBM per device.

```python
import math
import jax
import jax.numpy as jnp
import numpy as np
from jax import lax

D = 1024
HEADS = 16
HD = 64
FF = 4096
SEQ_LEN = 1024
MICRO = 2
SECTIONS = 2
TD = 256
TOKENS = 4096
EXPERT_TOTAL = 4
EXPERT_CAPACITY = 64


def steps_of(key, dims, split, least, high):
    def one(dim, shards_of):
        heights = jax.random.uniform(jax.random.fold_in(jax.random.fold_in(key, 6), dim), (shards_of,), jnp.float32, least / len(split), high / len(split))
        return jnp.repeat(jnp.exp(heights), dims[dim] // shards_of).reshape((-1,) + (1,) * (len(dims) - dim - 1))

    level = one(*split[0])
    for cut in split[1:]:
        level = level * one(*cut)
    return level


def profile(number_of, total, reach, lean):
    weights = [(1 << 20) // math.isqrt(grade ** lean) + 1 for grade in range(2, number_of + 1)]
    surplus, counts = total - reach - (number_of - 1), [1] * (number_of - 1)
    while surplus > 0:
        movable = [i for i in range(number_of - 1) if counts[i] < reach]
        whole, budget = sum([weights[i] for i in movable]), surplus
        for i in movable:
            more = min(reach - counts[i], max(1, budget * weights[i] // whole), surplus)
            counts[i] = counts[i] + more
            surplus = surplus - more
    return np.array([reach] + counts)


def ragged(own_key, number_of, total, reach, lean):
    if number_of == 2:
        one = jax.random.randint(own_key, (), max(1, total - reach), min(reach, total - 1) + 1)
        return jnp.stack([one, total - one])
    lengths = jnp.asarray(profile(number_of, total, reach, lean), jnp.int32)
    pairs = (number_of - 1) // 2
    donor, receiver = lengths[1:1 + 2 * pairs:2], lengths[2:2 + 2 * pairs:2]
    room = jnp.minimum(donor - 1, reach - receiver)
    moved = jax.random.randint(jax.random.fold_in(own_key, 1), (pairs,), 0, 1 << 20) % (room + 1)
    lengths = lengths.at[1:1 + 2 * pairs:2].set(donor - moved).at[2:2 + 2 * pairs:2].set(receiver + moved)
    return lengths[jax.random.permutation(jax.random.fold_in(own_key, 2), number_of)]


def deal_out(rng, own, number, rows, amount, top, reach, slope):
    sequence = jax.random.permutation(rng, amount)
    heavy_load, ordinary = portions_of(amount, rows * top, reach, slope, True), portions_of(amount, rows * top, reach, slope, False)
    places = jnp.arange(amount)

    def named(tallies, rotation):
        used = int((tallies > 0).sum())
        fixed = max(1, used // 4)
        moved = fixed + (places - fixed + rotation * (used - fixed)) % max(1, amount - fixed)
        return jnp.zeros((amount,), jnp.int32).at[sequence[jnp.where(places < fixed, places, moved)]].set(jnp.asarray(tallies, jnp.int32))

    tallies = jnp.where(number % 4 == 0, named(heavy_load, number // 4), named(ordinary, number - number // 4 - 1))
    mixed = jax.random.permutation(jax.random.fold_in(own, 3), amount)
    source_of, receiver = mixed[0:amount // 2 * 2:2], mixed[1:amount // 2 * 2:2]
    room = jnp.minimum(tallies[source_of] - 1, reach - tallies[receiver]) // 2
    room = jnp.where((source_of == sequence[0]) | (receiver == sequence[0]) | (tallies[receiver] == 0), 0, jnp.maximum(room, 0))
    moved = jax.random.randint(jax.random.fold_in(own, 4), (amount // 2,), 0, 1 << 20) % (room + 1)
    tallies = tallies.at[source_of].add(-moved).at[receiver].add(moved)
    labels = jnp.searchsorted(jnp.cumsum(tallies), jnp.arange(rows * top), side="right").astype(jnp.int32)
    grid = labels.reshape(top, rows).T
    grid = grid[jax.random.permutation(jax.random.fold_in(own, 1), rows)]
    rotation = jax.random.randint(jax.random.fold_in(own, 2), (rows, 1), 0, top)
    return jnp.take_along_axis(grid, (jnp.arange(top)[None, :] + rotation) % top, axis=1)


def portions_of(number_of, total, most, skew, full):
    loads = [(1 << 20) // math.isqrt(rank ** skew) + 1 for rank in range(1, number_of + 1)]
    largest = most if full else min(most, max(-(-total // number_of), total * loads[0] // sum(loads)))
    least = 1 if total - largest >= number_of - 1 else 0
    given, spare = [largest] + [least] * (number_of - 1), total - largest - least * (number_of - 1)
    while spare > 0:
        free = [i for i in range(1, number_of) if given[i] < largest] or [i for i in range(1, number_of) if given[i] < most]
        pool, left = sum([loads[i] for i in free]), spare
        for i in free:
            more = min(most - given[i], max(1, left * loads[i] // pool), spare)
            given[i] = given[i] + more
            spare = spare - more
    return np.array(given)


def bell_draw(key, dims, spread, reach, pieces=(), held_as=jnp.bfloat16):
    values = jax.random.normal(key, dims, jnp.float32) * spread
    if len(pieces) > 0:
        values = steps_of(key, dims, pieces, -0.22, 0.18) * values
    return jnp.clip(values, min=-reach, max=reach).astype(held_as)


def setup_inputs(seed: int = 0) -> dict:
    seeds = jax.random.split(jax.random.key(seed), 15)
    tokens_in = bell_draw(seeds[0], (MICRO, TOKENS, D), 1.0, 6.0, ((1, 16),))
    cotangent = bell_draw(seeds[1], (MICRO, TOKENS, D), 1.0, 6.0, ((1, 16),))
    segments = jax.vmap(lambda own: jnp.searchsorted(jnp.cumsum(ragged(own, TOKENS * 4 // SEQ_LEN, TOKENS, SEQ_LEN, 2)), jnp.arange(TOKENS), side="right"))(jax.random.split(seeds[2], MICRO)).reshape((MICRO, TOKENS)).astype(jnp.int32)
    routes_keys = jax.random.split(jax.random.fold_in(seeds[3], 1), SECTIONS * MICRO * TOKENS // TD)
    routes_turns = jax.random.permutation(jax.random.fold_in(seeds[3], 3), SECTIONS * MICRO * TOKENS // TD)
    routes = jax.vmap(lambda own, number: deal_out(jax.random.fold_in(seeds[3], 2), own, number, TD, EXPERT_TOTAL, 1, EXPERT_CAPACITY, 0))(routes_keys, routes_turns).reshape((SECTIONS, MICRO, TOKENS, 1))
    ln1_gain = jnp.clip(1.0 + 0.1 * jax.random.normal(seeds[4], (SECTIONS, D), jnp.float32), 0.5, 1.5)
    w_qkv = bell_draw(seeds[5], (SECTIONS, D, 3 * HEADS * HD), D ** -0.5, 0.1875, ((0, 2), (2, 4)))
    w_out = bell_draw(seeds[6], (SECTIONS, HEADS * HD, D), (max(1, HEADS * HD // 128)) ** -0.5, 2.0, ((0, 2), (1, 4)))
    ln2_gain = jnp.clip(1.0 + 0.1 * jax.random.normal(seeds[7], (SECTIONS, D), jnp.float32), 0.5, 1.5)
    w_up = bell_draw(seeds[8], (SECTIONS, D, FF), D ** -0.5, 0.1875, ((0, 2), (2, 4)))
    w_down = bell_draw(seeds[9], (SECTIONS, FF, D), FF ** -0.5, 0.09375, ((0, 2), (1, 4)))
    centroids = bell_draw(seeds[10], (SECTIONS, EXPERT_TOTAL, D), (2 * D) ** -0.5, 0.125, ((0, 2), (1, 4)))
    sub_gains = jnp.clip(1.0 + 0.1 * jax.random.normal(seeds[11], (SECTIONS, EXPERT_TOTAL, 2, D), jnp.float32), 0.5, 1.5)
    expert_up = bell_draw(seeds[12], (SECTIONS, EXPERT_TOTAL, 2, D, FF), D ** -0.5, 0.1875, ((0, 2), (1, 4), (4, 4)))
    expert_down = bell_draw(seeds[13], (SECTIONS, EXPERT_TOTAL, 2, FF, D), FF ** -0.5, 0.09375, ((0, 2), (1, 4), (3, 4)))
    return dict(tokens_in=tokens_in, cotangent=cotangent, segments=segments, routes=routes, ln1_gain=ln1_gain, w_qkv=w_qkv, w_out=w_out, ln2_gain=ln2_gain, w_up=w_up, w_down=w_down, centroids=centroids, sub_gains=sub_gains, expert_up=expert_up, expert_down=expert_down)


epsilon = 1e-05
highest_prec = lax.Precision.HIGHEST

@jax.custom_vjp
def low(v):
    return lax.optimization_barrier(v.astype(jnp.bfloat16)).astype(jnp.float32)

@jax.custom_vjp
def low_back(v):
    return v

def low_keep(v):
    return (low(v), None)

def low_pass(kept, grad):
    return (grad,)

def back_keep(v):
    return (v, None)

def back_low(kept, grad):
    return (low(grad),)
low.defvjp(low_keep, low_pass)
low_back.defvjp(back_keep, back_low)

def matmul_high(first_arg, second_arg):
    return jnp.dot(first_arg, second_arg, precision=highest_prec)

def gelu_curve(values):
    return 0.5 * values * (1.0 + lax.erf(values * (1.0 / math.sqrt(2.0))))

def layer_norm(values, gain_vec):
    center = values - lax.optimization_barrier(jnp.mean(values, axis=-1, keepdims=True))
    variance = lax.optimization_barrier(jnp.mean(center * center, axis=-1, keepdims=True))
    return center * lax.rsqrt(variance + epsilon) * gain_vec

def attend_sequence(seq_pair):
    packed, seg_row = seq_pair
    head_parts = packed.reshape(SEQ_LEN, HEADS, 3, HD)
    queries = head_parts[:, :, 0]
    keys_all = head_parts[:, :, 1]
    values_all = head_parts[:, :, 2]
    positions = jnp.arange(SEQ_LEN, dtype=jnp.int32)
    allowed = (positions[:, None] >= positions[None, :]) & (seg_row[:, None] == seg_row[None, :])
    scores = low_back(jnp.einsum('qhd,khd->hqk', queries, keys_all, precision=highest_prec) * (1.0 / math.sqrt(HD)))
    scores = jnp.where(allowed[None], scores, -1e+30)
    probabilities = low(jax.nn.softmax(scores, axis=-1))
    attended = jnp.einsum('hqk,khd->qhd', probabilities, values_all, precision=highest_prec)
    return attended.reshape(SEQ_LEN, HEADS * HD)

def apply_expert_layer(expert_pack):
    rows_in, cent_row, gain_rows, up_mats, down_mats = expert_pack
    gate_value = jax.nn.sigmoid(jnp.dot(rows_in, cent_row, precision=highest_prec))
    current = rows_in
    for sublayer in range(2):
        normed = low(layer_norm(current, gain_rows[sublayer]))
        activated = low(gelu_curve(low_back(matmul_high(normed, up_mats[sublayer]))))
        current = current + low_back(matmul_high(activated, down_mats[sublayer]))
    return gate_value[:, None] * current + (1.0 - gate_value[:, None]) * rows_in

def expert_layer_block(dense_output, routing_row, centroid_weight, sublayer_weight, expert_up_weight, expert_down_weight):
    starting_rows = low(low_back(dense_output))
    source_list = routing_row.shape[0] // TD
    grouped = routing_row.reshape(source_list, TD)
    onehot = (grouped[:, :, None] == jnp.arange(EXPERT_TOTAL, dtype=jnp.int32)[None, None, :]).astype(jnp.int32)
    rank_ids = lax.optimization_barrier(jnp.sum(jnp.cumsum(onehot, axis=1) * onehot, axis=2)) - 1
    slot_ids = (grouped * (source_list * EXPERT_CAPACITY) + jnp.arange(source_list, dtype=jnp.int32)[:, None] * EXPERT_CAPACITY + rank_ids).reshape(-1).astype(jnp.int32)
    holding_buffer = jnp.zeros((EXPERT_TOTAL * source_list * EXPERT_CAPACITY, starting_rows.shape[1]), jnp.float32).at[slot_ids].set(starting_rows)
    result_list = lax.map(jax.checkpoint(apply_expert_layer), (holding_buffer.reshape(EXPERT_TOTAL, source_list * EXPERT_CAPACITY, starting_rows.shape[1]), centroid_weight, sublayer_weight, expert_up_weight, expert_down_weight))
    return low(result_list.reshape(EXPERT_TOTAL * source_list * EXPERT_CAPACITY, starting_rows.shape[1])[slot_ids])

def section_layer(hidden, segment_row, routing_row, weight_collection):
    first_norm_gain, query_key_value_weight, output_weight, second_norm_gain, up_weight, down_weight, centroid_weight, sublayer_weight, expert_up_weight, expert_down_weight = weight_collection
    normed = low(layer_norm(hidden, first_norm_gain))
    packed = low(low_back(matmul_high(normed, query_key_value_weight)))
    sequences = packed.reshape(-1, SEQ_LEN, packed.shape[1])
    seg_rows = segment_row.reshape(-1, SEQ_LEN)
    attended = lax.map(jax.checkpoint(attend_sequence), (sequences, seg_rows))
    attended = low(low_back(attended.reshape(hidden.shape[0], HEADS * HD)))
    middle = hidden + low_back(matmul_high(attended, output_weight))
    normed_two = low(layer_norm(middle, second_norm_gain))
    activated = low(gelu_curve(low_back(matmul_high(normed_two, up_weight))))
    dense_output = middle + low_back(matmul_high(activated, down_weight))
    return expert_layer_block(dense_output, routing_row, centroid_weight, sublayer_weight, expert_up_weight, expert_down_weight)

def reference(tokens_in, cotangent, segments, routes, ln1_gain, w_qkv, w_out, ln2_gain, w_up, w_down, centroids, sub_gains, expert_up, expert_down):
    params = tuple((weight_arr.astype(jnp.float32) for weight_arr in (ln1_gain, w_qkv, w_out, ln2_gain, w_up, w_down, centroids, sub_gains, expert_up, expert_down)))

    def forward(inputs, *weights):
        result_list = []
        for batch_no in range(MICRO):
            hidden = inputs[batch_no]
            for section_no in range(SECTIONS):
                if section_no > 0:
                    hidden = low_back(hidden)
                weight_collection = tuple((weight_arr[section_no] for weight_arr in weights))
                hidden = section_layer(hidden, segments[batch_no], routes[section_no, batch_no, :, 0], weight_collection)
            result_list.append(hidden)
        return jnp.stack(result_list)
    outputs, pullback = jax.vjp(forward, tokens_in.astype(jnp.float32), *params)
    grads = pullback(cotangent.astype(jnp.float32))
    return (outputs.astype(jnp.bfloat16), grads[0], grads[1], grads[2], grads[3], grads[4], grads[5], grads[6], grads[7], grads[8], grads[9], grads[10])
```

```python
import functools
import math

import jax
import jax.numpy as jnp
from jax import lax
from jax.experimental import pallas as pl
from jax.experimental.pallas import tpu as pltpu
from jax.sharding import PartitionSpec as P

HD = 64
SEQ_LEN = 1024


epsilon = 1e-05
root_half = 1.0 / math.sqrt(2.0)
root_tau = 1.0 / math.sqrt(2.0 * math.pi)
masked_score = -1e30
highest_prec = lax.Precision.HIGHEST


def section_swap(value):
    return lax.ppermute(value, "section", [(0, 1), (1, 0)])


def section_send(value, source):
    return lax.ppermute(value, "section", [(source, 1 - source)])


def together(values):
    return lax.optimization_barrier(values)


def after(value, earlier):
    return lax.optimization_barrier((value, earlier))[0]


def low(value):
    return value.astype(jnp.bfloat16)


def matmul(first_arg, second_arg):
    return jnp.dot(first_arg, second_arg, preferred_element_type=jnp.float32)


def matmul_left(first_arg, second_arg):
    return lax.dot_general(
        first_arg, second_arg, (((0,), (0,)), ((), ())), preferred_element_type=jnp.float32
    )


def matmul_right(first_arg, second_arg):
    return lax.dot_general(
        first_arg, second_arg, (((1,), (1,)), ((), ())), preferred_element_type=jnp.float32
    )


def hidden_tile(width):
    return min(512, width)


def row_steps(rows):
    step = min(256, rows)
    return [pl.ds(i, step) for i in range(0, rows, step)]


def store_parts(total, parts):
    size = parts[0].shape[0]
    for i, part in enumerate(parts):
        part[...] = total[pl.ds(i * size, size), :].astype(part.dtype)


def on_each_set(sets, steps, work):
    if len(sets) == 1:
        work(*sets[0])
        return
    for i, tiles in enumerate(sets):

        @pl.when(pl.program_id(0) // steps == i)
        def _(tiles=tiles):
            work(*tiles)


def mlp_forward_kernel(count, moves, sets, set_steps, *refs):
    blocks, refs = refs[:count], refs[count:]
    weights, refs = refs[: 2 * sets], refs[2 * sets :]
    weights = list(zip(weights[::2], weights[1::2]))
    if moves:
        moving, own_moving, middle, refs = refs[0], refs[1], refs[2], refs[3:]
    act, slope, rows_out = refs[:3]
    parts, total = refs[3:-1], refs[-1]
    step = pl.program_id(0)
    size = blocks[0].shape[0]
    steps = row_steps(total.shape[0])

    @pl.when(step == 0)
    def _():
        for i in range(count):
            rows_out[pl.ds(i * size, size), :] = blocks[i][...]
        if moves:
            for span in steps:
                total[span, :] = matmul(own_moving[span, :], middle[...])
        else:
            total[...] = jnp.zeros_like(total)

    def work(up_tile, down_tile):
        for span in steps:
            pre = matmul(rows_out[span, :], up_tile[...])
            below = 0.5 * (1.0 + lax.erf(pre * root_half))
            act[span, :] = low(pre * below)
            slope[span, :] = low(below + pre * (jnp.exp(-0.5 * pre * pre) * root_tau))
            if not moves:
                total[span, :] += matmul(act[span, :], down_tile[...])
        if moves:
            for span in steps:
                total[span, :] += matmul(low(matmul(moving[span, :], act[...])), down_tile[...])

    on_each_set(weights, set_steps, work)

    @pl.when(step == pl.num_programs(0) - 1)
    def _():
        store_parts(total, parts)


def mlp_backward_kernel(count, moves, sets, set_steps, *refs):
    blocks, slope, refs = refs[:count], refs[count], refs[count + 1 :]
    weights, refs = refs[: 2 * sets], refs[2 * sets :]
    weights = list(zip(weights[::2], weights[1::2]))
    if moves:
        moving, refs = refs[0], refs[1:]
    grad_pre, rows_out = refs[:2]
    parts, total = refs[2:-1], refs[-1]
    size = blocks[0].shape[0]
    steps = row_steps(total.shape[0])

    @pl.when(pl.program_id(0) == 0)
    def _():
        if moves:
            for span in steps:
                moved = jnp.zeros((span.size, total.shape[1]), jnp.float32)
                for i in range(count):
                    moved += matmul_left(moving[pl.ds(i * size, size), span], blocks[i][...])
                rows_out[span, :] = low(moved)
        else:
            for i in range(count):
                rows_out[pl.ds(i * size, size), :] = blocks[i][...]
        total[...] = jnp.zeros_like(total)

    def work(up_tile, down_tile):
        for span in steps:
            grad_act = matmul_right(rows_out[span, :], down_tile[...])
            grad_pre[span, :] = low(grad_act * slope[span, :].astype(jnp.float32))
            total[span, :] += matmul_right(grad_pre[span, :], up_tile[...])

    on_each_set(weights, set_steps, work)

    @pl.when(pl.program_id(0) == pl.num_programs(0) - 1)
    def _():
        store_parts(total, parts)


def mlp_call(kernel, blocks, streamed, resident, hidden_outs, weights):
    count, size = len(blocks), blocks[0].shape[0]
    rows, width = count * size, blocks[0].shape[1]
    set_width = weights[0][0].shape[-1]
    hidden = set_width * len(weights)
    tile = hidden_tile(set_width)
    set_steps = set_width // tile

    def whole(shape):
        return pl.BlockSpec(shape, lambda i: (0,) * len(shape))

    def tiles(lead, set_no, along_rows):
        def index(i):
            turn = jnp.clip(i - set_no * set_steps, 0, set_steps - 1)
            return lead + ((turn, 0) if along_rows else (0, turn))

        shape = (tile, width) if along_rows else (width, tile)
        return pl.BlockSpec((None,) * len(lead) + shape, index)

    columns = pl.BlockSpec((rows, tile), lambda i: (0, i))
    own_type = jnp.float32 if count > 1 else jnp.bfloat16
    part_types = [own_type] + [jnp.bfloat16] * (count - 1)
    weight_specs, matrices = ([], [])
    for set_no, (up_mat, up_lead, down_mat, down_lead) in enumerate(weights):
        weight_specs += [tiles(up_lead, set_no, False), tiles(down_lead, set_no, True)]
        matrices += [up_mat, down_mat]
    outs = pl.pallas_call(
        functools.partial(kernel, count, len(resident) > 0, len(weights), set_steps),
        grid=(hidden // tile,),
        in_specs=[whole(block.shape) for block in blocks]
        + [columns for _ in streamed]
        + weight_specs
        + [whole(arr.shape) for arr in resident],
        out_shape=[jax.ShapeDtypeStruct((rows, hidden), jnp.bfloat16)] * hidden_outs
        + [jax.ShapeDtypeStruct((rows, width), jnp.bfloat16)]
        + [jax.ShapeDtypeStruct((size, width), kind) for kind in part_types],
        out_specs=[columns] * hidden_outs
        + [whole((rows, width))]
        + [whole((size, width)) for _ in part_types],
        scratch_shapes=[pltpu.VMEM((rows, width), jnp.float32)],
        compiler_params=pltpu.CompilerParams(vmem_limit_bytes=40 * 2**20),
        cost_estimate=pl.CostEstimate(
            flops=4 * rows * width * hidden,
            bytes_accessed=4 * width * hidden + 6 * rows * width,
            transcendentals=2 * rows * hidden,
        ),
    )(*blocks, *streamed, *matrices, *resident)
    return outs[:hidden_outs], outs[hidden_outs], outs[hidden_outs + 1 :]


def mlp_forward(blocks, weights, moved=()):
    (act, slope), rows, parts = mlp_call(mlp_forward_kernel, blocks, (), moved, 2, weights)
    return (parts, (rows, act, slope))


def mlp_backward(blocks, slope, weights, moved=()):
    (grad_pre,), rows, parts = mlp_call(mlp_backward_kernel, blocks, (slope,), moved, 1, weights)
    return (parts, rows, grad_pre)


def norm_forward(values, gain_vec):
    center = values - jnp.mean(values, axis=-1, keepdims=True)
    scale_inv = lax.rsqrt(jnp.mean(center * center, axis=-1, keepdims=True) + epsilon)
    normal = center * scale_inv
    return (normal * gain_vec, normal, scale_inv)


def norm_backward(grad_out, normal, scale_inv, gain_vec):
    scaled = grad_out * gain_vec
    grad_values = scale_inv * (
        scaled
        - jnp.mean(scaled, axis=-1, keepdims=True)
        - normal * jnp.mean(scaled * normal, axis=-1, keepdims=True)
    )
    return (grad_values, jnp.sum(grad_out * normal, axis=0))


def is_square(axis):
    return lax.axis_size(axis) == 4


def wide_hop(value, mask):
    return lax.ppermute(value, "wide", [(i, i ^ mask) for i in range(4)])


def wide_spread(rows):
    if not is_square("wide"):
        return [lax.all_gather(rows, "wide", axis=0, tiled=True)]
    half = rows.shape[0] // 2
    y_first = wide_hop(rows[:half], 2)
    x_last = wide_hop(rows[half:], 1)
    y_last = wide_hop(rows[half:], 2)
    x_first = wide_hop(rows[:half], 1)
    d_first = wide_hop(y_first, 1)
    d_last = wide_hop(x_last, 2)
    return [
        rows,
        jnp.concatenate([x_first, x_last]),
        jnp.concatenate([y_first, y_last]),
        jnp.concatenate([d_first, d_last]),
    ]


def wide_collect(parts):
    if not is_square("wide"):
        return lax.psum_scatter(low(parts[0]), "wide", scatter_dimension=0, tiled=True).astype(
            jnp.float32
        )
    own = parts[0]
    x_part, y_part, d_low = [low(part) for part in parts[1:]]
    half = own.shape[0] // 2
    via_x = wide_hop(d_low[:half], 1)
    via_y = wide_hop(d_low[half:], 2)
    x_first = wide_hop(x_part[:half], 1)
    y_last = wide_hop(y_part[half:], 2)
    y_first = wide_hop(y_part[:half] + via_x, 2)
    x_last = wide_hop(x_part[half:] + via_y, 1)
    first = own[:half] + x_first.astype(jnp.float32) + y_first.astype(jnp.float32)
    last = own[half:] + x_last.astype(jnp.float32) + y_last.astype(jnp.float32)
    return jnp.concatenate([first, last])


def in_order(blocks):
    if len(blocks) == 1:
        return blocks[0]
    me = lax.axis_index("wide")
    stacked = jnp.stack(blocks)
    return jnp.concatenate(
        [lax.dynamic_index_in_dim(stacked, me ^ i, 0, keepdims=False) for i in range(4)]
    )


def in_blocks(values):
    if not is_square("wide"):
        return [values]
    me = lax.axis_index("wide")
    size = values.shape[0] // 4
    return [lax.dynamic_slice_in_dim(values, (me ^ i) * size, size, 0) for i in range(4)]


def expert_trade(values):
    return lax.all_to_all(values, "wide", split_axis=0, concat_axis=0, tiled=True)


def rep_hop(value, mask):
    return lax.ppermute(value, "rep", [(i, i ^ mask) for i in range(4)])


rep_pairs = [[0, 1], [2, 3]]


def rep_pair_gather(values):
    return lax.all_gather(values, "rep", axis=0, tiled=True, axis_index_groups=rep_pairs)


def rep_pair_scatter(values):
    return lax.psum_scatter(
        values, "rep", scatter_dimension=0, tiled=True, axis_index_groups=rep_pairs
    )


def rep_spread(rows):
    return [rows, rep_hop(rows, 2)]


def rep_collect(parts):
    return parts[0] + rep_hop(parts[1], 2).astype(jnp.float32)


def small_scatter(values, axis):
    if not is_square(axis):
        return lax.psum_scatter(values, axis, scatter_dimension=1, tiled=True)
    me = lax.axis_index(axis)
    size = values.shape[1] // 4

    def columns(device):
        return lax.dynamic_slice_in_dim(values, device * size, size, 1)

    total = columns(me)
    for mask in (1, 2, 3):
        pairs = [(i, i ^ mask) for i in range(4)]
        total = total + lax.ppermute(columns(me ^ mask), axis, pairs)
    return total


def joined(blocks):
    return blocks[0] if len(blocks) == 1 else jnp.concatenate(blocks)


def attention_layout(packed, segment_ids):
    row_count = packed.shape[0]
    head_count = packed.shape[1] // (3 * HD)
    seq_count = row_count // SEQ_LEN
    block_rows = min(512, SEQ_LEN)
    per_seq = SEQ_LEN // block_rows
    head_parts = packed.reshape(seq_count, SEQ_LEN, head_count, 3, HD)
    seg_table = segment_ids.reshape(seq_count, SEQ_LEN)
    return (head_parts, seg_table, block_rows, per_seq, head_count, seq_count)


def block_scores(seq_parts, seq_segs, row_start, block_rows):
    key_end = row_start + block_rows
    queries = seq_parts[row_start:key_end, :, 0]
    scores = jnp.einsum(
        "qhd,khd->hqk", queries, seq_parts[:key_end, :, 1], preferred_element_type=jnp.float32
    ) * (1.0 / math.sqrt(HD))
    seg_query = seq_segs[row_start:key_end]
    query_pos = row_start + jnp.arange(block_rows, dtype=jnp.int32)
    key_pos = jnp.arange(key_end, dtype=jnp.int32)
    allowed = (query_pos[:, None] >= key_pos[None, :]) & (
        seg_query[:, None] == seq_segs[None, :key_end]
    )
    return (jnp.where(allowed[None], scores, masked_score), queries)


def attention_forward(packed, segment_ids):
    head_parts, seg_table, block_rows, per_seq, head_count, seq_count = attention_layout(
        packed, segment_ids
    )

    def one_seq(seq_pack):
        seq_parts, seq_segs = seq_pack
        block_outs, block_logs = ([], [])
        for block_no in range(per_seq):
            row_start = block_no * block_rows
            key_end = row_start + block_rows
            scores, queries = block_scores(seq_parts, seq_segs, row_start, block_rows)
            highest = jnp.max(scores, axis=-1, keepdims=True)
            exponent = jnp.exp(scores - highest)
            row_total = jnp.sum(exponent, axis=-1, keepdims=True)
            probs_low = (exponent / row_total).astype(jnp.bfloat16)
            attended = jnp.einsum(
                "hqk,khd->qhd",
                probs_low,
                seq_parts[:key_end, :, 2],
                preferred_element_type=jnp.float32,
            )
            block_outs.append(attended.astype(jnp.bfloat16).reshape(block_rows, head_count * HD))
            block_logs.append(highest[..., 0] + jnp.log(row_total[..., 0]))
        return (jnp.concatenate(block_outs, axis=0), jnp.stack(block_logs))

    attended, log_totals = lax.map(one_seq, (head_parts, seg_table))
    return (attended.reshape(packed.shape[0], head_count * HD), log_totals)


def attention_backward(packed, segment_ids, log_totals, grad_att):
    head_parts, seg_table, block_rows, per_seq, head_count, seq_count = attention_layout(
        packed, segment_ids
    )
    grad_seqs = grad_att.reshape(seq_count, SEQ_LEN, head_count, HD)
    scale_value = 1.0 / math.sqrt(HD)

    def one_seq(seq_pack):
        seq_parts, seq_segs, seq_logs, seq_grad = seq_pack
        query_list = []
        grad_key = jnp.zeros((SEQ_LEN, head_count, HD), jnp.float32)
        grad_value = jnp.zeros((SEQ_LEN, head_count, HD), jnp.float32)
        for block_no in range(per_seq):
            row_start = block_no * block_rows
            key_end = row_start + block_rows
            scores, queries = block_scores(seq_parts, seq_segs, row_start, block_rows)
            probs = jnp.exp(scores - seq_logs[block_no][..., None])
            grad_here = seq_grad[row_start:key_end]
            grad_probs = jnp.einsum(
                "qhd,khd->hqk",
                grad_here,
                seq_parts[:key_end, :, 2],
                preferred_element_type=jnp.float32,
            )
            inner = jnp.sum(grad_probs * probs, axis=-1, keepdims=True)
            grad_scores = (probs * (grad_probs - inner)).astype(jnp.bfloat16)
            query_list.append(
                jnp.einsum(
                    "hqk,khd->qhd",
                    grad_scores,
                    seq_parts[:key_end, :, 1],
                    preferred_element_type=jnp.float32,
                )
                * scale_value
            )
            key_part = (
                jnp.einsum("hqk,qhd->khd", grad_scores, queries, preferred_element_type=jnp.float32)
                * scale_value
            )
            value_part = jnp.einsum(
                "hqk,qhd->khd",
                probs.astype(jnp.bfloat16),
                grad_here,
                preferred_element_type=jnp.float32,
            )
            pad_rows = ((0, SEQ_LEN - key_end), (0, 0), (0, 0))
            grad_key = grad_key + jnp.pad(key_part, pad_rows)
            grad_value = grad_value + jnp.pad(value_part, pad_rows)
        return (jnp.concatenate(query_list, axis=0), grad_key, grad_value)

    grad_query, grad_key, grad_value = lax.map(
        one_seq, (head_parts, seg_table, log_totals, grad_seqs)
    )
    stacked = jnp.stack([grad_query, grad_key, grad_value], axis=3)
    return stacked.reshape(packed.shape[0], head_count * 3 * HD).astype(jnp.bfloat16)


class RowOrder:
    def __init__(self, place):
        self.place = place
        self.count = place.shape[0]

    def onehot(self):
        rows = jnp.arange(self.count, dtype=jnp.int32)
        return (self.place[:, None] == rows[None, :]).astype(jnp.bfloat16)

    def to_tokens(self, rows):
        return low(matmul(self.onehot(), rows))

    def from_tokens(self, tokens):
        return low(matmul_left(self.onehot(), tokens))


def token_order(count):
    tokens = jnp.arange(count, dtype=jnp.int32)
    if not is_square("wide"):
        return RowOrder(tokens)
    return RowOrder(tokens ^ (lax.axis_index("wide") * (count // 4)))


def wide_table(values):
    if not is_square("wide"):
        return lax.all_gather(values, "wide", axis=0)
    me = lax.axis_index("wide")
    hops = jnp.stack([values] + [wide_hop(values, mask) for mask in (1, 2, 3)])
    return jnp.stack([lax.dynamic_index_in_dim(hops, me ^ i, 0, keepdims=False) for i in range(4)])


def routed_order(all_routes):
    devices, size = all_routes.shape
    experts = jnp.arange(devices, dtype=jnp.int32)
    tokens = jnp.arange(size, dtype=jnp.int32)
    same = (all_routes[:, :, None] == all_routes[:, None, :]) & (tokens[:, None] > tokens[None, :])
    rank_ids = jnp.sum(same.astype(jnp.int32), axis=2)
    owner = all_routes ^ lax.axis_index("wide") if is_square("wide") else all_routes
    place = owner * size + experts[:, None] * (size // devices) + rank_ids
    return RowOrder(place.reshape(-1))


def order_change(source, target):
    rows = jnp.arange(target.count, dtype=jnp.int32)
    found = (target.place[:, None] == rows[None, :]).astype(jnp.int32)
    return jnp.sum(found * source.place[:, None], axis=0)


def split(values):
    if not is_square("wide"):
        return [values]
    size = values.shape[0] // 4
    return [values[i * size : (i + 1) * size] for i in range(4)]


def own_start(size):
    return 0 if is_square("wide") else lax.axis_index("wide") * size


def dense_forward(block_in, segment_ids, weights, order, change):
    first_norm_gain, qkv_mat, out_mat, second_norm_gain, mlp_weights = weights
    own_size = block_in.shape[0]
    shaped_one, normal_one, inv_one = norm_forward(block_in, first_norm_gain)
    first_blocks = wide_spread(low(shaped_one))
    packed = order.to_tokens(joined([low(matmul(rows, qkv_mat)) for rows in first_blocks]))
    attended, log_totals = attention_forward(packed, segment_ids)
    attended = order.from_tokens(attended)
    middle = block_in + wide_collect([matmul(rows, out_mat) for rows in split(attended)])
    shaped_two, normal_two, inv_two = norm_forward(middle, second_norm_gain)
    second_blocks = wide_spread(low(shaped_two))
    rows = jnp.arange(change.shape[0], dtype=jnp.int32)
    moving = (change[:, None] == rows[None, :]).astype(jnp.bfloat16)
    own_rows = own_start(own_size) + jnp.arange(own_size, dtype=jnp.int32)
    own_moving = (change[:, None] == own_rows[None, :]).astype(jnp.bfloat16)
    parts, mlp_saved = mlp_forward(second_blocks, mlp_weights, (moving, own_moving, low(middle)))
    return (
        wide_collect(parts),
        (
            normal_one,
            inv_one,
            first_blocks,
            packed,
            attended,
            log_totals,
            normal_two,
            inv_two,
            mlp_saved,
            moving,
        ),
    )


def dense_backward(grad_rows, saved_state, segment_ids, weights, order, sums, last_part, finish):
    first_norm_gain, qkv_mat, out_mat, second_norm_gain, mlp_weights = weights
    (
        normal_one,
        inv_one,
        first_blocks,
        packed,
        attended,
        log_totals,
        normal_two,
        inv_two,
        (second_rows, activated, slope),
        moving,
    ) = saved_state
    own_size = grad_rows.shape[0]
    blocks, sums, last_part = together((wide_spread(grad_rows), sums, last_part))
    last_sum = rep_pair_scatter(last_part)
    parts, grad_wide, grad_pre = mlp_backward(blocks, slope, mlp_weights, (moving,))
    grad_out = lax.dynamic_slice_in_dim(grad_wide, own_start(own_size), own_size, 0)
    grad_norm_two = wide_collect(parts)
    down_part = half_summed(weight_grad([activated], [grad_wide]), 0)
    up_part = half_summed(weight_grad([second_rows], [grad_pre]), 1)
    grad_norm_two, down_part, up_part = together((grad_norm_two, down_part, up_part))
    grad_down, grad_up = rep_summed(down_part, 1), rep_summed(up_part, 0)
    grad_in_two, grad_gain_two = norm_backward(grad_norm_two, normal_two, inv_two, second_norm_gain)
    grad_middle = grad_out.astype(jnp.float32) + grad_in_two
    mid_blocks, last_sum = together((wide_spread(low(grad_middle)), last_sum))
    finished = finish([last_sum, sums])
    grad_att = order.to_tokens(joined([low(matmul_right(rows, out_mat)) for rows in mid_blocks]))
    grad_packed = attention_backward(packed, segment_ids, log_totals, grad_att)
    out_part = half_summed(low(matmul_left(attended, joined(mid_blocks))), 0)
    grad_packed, out_part, grad_down, grad_up = together(
        (grad_packed, out_part, grad_down, grad_up)
    )
    grad_packed = order.from_tokens(grad_packed)
    grad_norm_one = wide_collect([matmul_right(rows, qkv_mat) for rows in split(grad_packed)])
    qkv_part = half_summed(low(matmul_left(joined(first_blocks), grad_packed)), 1)
    grad_out_mat = rep_summed(out_part, 1)
    grad_norm_one, qkv_part, finished, grad_out_mat = together(
        (grad_norm_one, qkv_part, finished, grad_out_mat)
    )
    grad_qkv = rep_summed(qkv_part, 0)
    grad_in_one, grad_gain_one = norm_backward(grad_norm_one, normal_one, inv_one, first_norm_gain)
    return (
        grad_middle + grad_in_one,
        (grad_gain_one, grad_qkv, grad_out_mat, grad_gain_two, grad_up, grad_down),
        finished,
    )


def half_summed(partial, dim):
    section = lax.axis_index("section")
    size = partial.shape[dim] // 2
    kept = lax.dynamic_slice_in_dim(partial, section * size, size, dim)
    given = lax.dynamic_slice_in_dim(partial, (1 - section) * size, size, dim)
    return low(kept.astype(jnp.float32) + section_swap(given).astype(jnp.float32))


def rep_summed(partial, dim):
    return lax.psum_scatter(partial, "rep", scatter_dimension=dim, tiled=True)


def both_halves(layer_halves, dim):
    is_first = lax.axis_index("section") == 0
    first, second = layer_halves
    kept = jnp.where(is_first, first, second)
    moved = section_swap(jnp.where(is_first, second, first))
    parts = [jnp.where(is_first, kept, moved), jnp.where(is_first, moved, kept)]
    return jnp.concatenate(parts, axis=dim).astype(jnp.float32)


def slot_matrix_of(route_ids):
    expert_count = lax.axis_size("wide")
    capacity = max(2, route_ids.shape[0] // expert_count)
    onehot = (route_ids[:, None] == jnp.arange(expert_count, dtype=jnp.int32)[None, :]).astype(
        jnp.int32
    )
    rank_ids = jnp.sum(jnp.cumsum(onehot, axis=0) * onehot, axis=1) - 1
    position = route_ids * capacity + rank_ids
    return (
        position[:, None] == jnp.arange(expert_count * capacity, dtype=jnp.int32)[None, :]
    ).astype(jnp.bfloat16)


def weight_grad_kernel(count, *refs):
    rows, grads, out = refs[:count], refs[count:-1], refs[-1]
    total = matmul_left(rows[0][...], grads[0][...])
    for row, grad in zip(rows[1:], grads[1:]):
        total += matmul_left(row[...], grad[...])
    out[...] = low(total)


def weight_grad(rows, grads, rows_half=None, columns_half=None):
    height, width = rows[0].shape[1], grads[0].shape[1]
    if rows_half is not None:
        height = height // 2
    if columns_half is not None:
        width = width // 2
    tile = hidden_tile(height)
    first, column = (rows_half or 0) * (height // tile), columns_half or 0
    depth = sum(arr.shape[0] for arr in rows)
    return pl.pallas_call(
        functools.partial(weight_grad_kernel, len(rows)),
        grid=(height // tile,),
        in_specs=[pl.BlockSpec((arr.shape[0], tile), lambda i: (0, i + first)) for arr in rows]
        + [pl.BlockSpec((arr.shape[0], width), lambda i: (0, column)) for arr in grads],
        out_shape=jax.ShapeDtypeStruct((height, width), jnp.bfloat16),
        out_specs=pl.BlockSpec((tile, width), lambda i: (i, 0)),
        compiler_params=pltpu.CompilerParams(vmem_limit_bytes=24 * 2**20),
        cost_estimate=pl.CostEstimate(
            flops=2 * depth * height * width,
            bytes_accessed=2 * (depth * (height + width) + height * width),
            transcendentals=0,
        ),
    )(*rows, *grads)


def chunked(values):
    half = values.shape[0] // 2
    return [values[:half], values[half:]]


def expert_forward(rows_in, centroid, gain_rows, mlp_weights):
    hidden, saved = ([], [])
    starts = [low(rows) for rows in chunked(rows_in)]
    states = [rows.astype(jnp.float32) for rows in starts]
    sublayer_saved = []
    for sublayer in range(2):
        kept = []
        for i, current in enumerate(states):
            shaped, normal, scale_inv = norm_forward(current, gain_rows[sublayer])
            shaped = low(shaped)
            blocks = rep_spread(shaped)
            parts, mlp_saved = mlp_forward(blocks, mlp_weights(sublayer))
            kept.append((normal, scale_inv, mlp_saved))
            states[i] = current + rep_collect(parts)
        sublayer_saved.append(kept)
    for arrived, current in zip(starts, states):
        starting_rows = arrived.astype(jnp.float32)
        gate_value = jax.nn.sigmoid(jnp.dot(arrived, centroid, preferred_element_type=jnp.float32))
        gate = gate_value[:, None]
        hidden.append(low(gate * current + (1.0 - gate) * starting_rows))
        saved.append((arrived, gate_value, current))
    return (jnp.concatenate(hidden), (saved, sublayer_saved))


def expert_backward(grad_rows, saved_state, centroid, gain_rows, mlp_weights, mid):
    saved, sublayer_saved = saved_state
    states, start_grads = ([], [])
    grad_centroid = jnp.zeros(centroid.shape, jnp.float32)
    for rows, (arrived, gate_value, final_state) in zip(chunked(grad_rows), saved):
        starting_rows = arrived.astype(jnp.float32)
        grad_mixed = rows.astype(jnp.float32)
        grad_gate = jnp.sum(grad_mixed * (final_state - starting_rows), axis=-1)
        grad_logit = grad_gate * gate_value * (1.0 - gate_value)
        grad_centroid += jnp.dot(grad_logit, starting_rows, precision=highest_prec)
        states.append(gate_value[:, None] * grad_mixed)
        start_grads.append(
            (1.0 - gate_value[:, None]) * grad_mixed
            + grad_logit[:, None] * centroid.astype(jnp.float32)[None, :]
        )
    gain_list, weight_grads = ([], [])
    for sublayer in (1, 0):
        collected, pieces = ([], [])
        for i, (_, _, (rows, act, slope)) in enumerate(sublayer_saved[sublayer]):
            given = low(states[i])
            blocks = rep_spread(given)
            parts, grad_wide, grad_pre = mlp_backward(blocks, slope, mlp_weights(sublayer))
            collected.append(rep_collect(parts))
            pieces.append((act, grad_wide, rows, grad_pre))
        if sublayer == 0:
            collected[0], weight_grads, mid = together((collected[0], weight_grads, mid))
            weight_grads = [rep_pair_scatter(part) for part in weight_grads]
        acts, grads_wide, rows, grads_pre = zip(*pieces)
        weight_grads.append(pair_weight_grads(rows, grads_pre, acts, grads_wide))
        gain = 0.0
        for i, (normal, scale_inv, _) in enumerate(sublayer_saved[sublayer]):
            grad_values, grad_gain = norm_backward(
                collected[i], normal, scale_inv, gain_rows[sublayer]
            )
            gain += grad_gain
            states[i] = states[i] + grad_values
        gain_list.append(gain)
    grad_start = jnp.concatenate([low(a + b) for a, b in zip(start_grads, states)])
    return (grad_start, (grad_centroid, gain_list[::-1]), weight_grads[::-1], mid)


def pair_weight_kernel(count, prefetched, *refs):
    rows, grads_pre, acts, grads_wide = [refs[i * count : (i + 1) * count] for i in range(4)]
    kept, given = refs[4 * count :]
    which = pl.program_id(0) ^ prefetched[0]

    def write(lefts, rights):
        total = matmul_left(lefts[0][...], rights[0][...])
        for left, right in zip(lefts[1:], rights[1:]):
            total += matmul_left(left[...], right[...])

        @pl.when(pl.program_id(0) == 0)
        def _():
            kept[...] = low(total)

        @pl.when(pl.program_id(0) == 1)
        def _():
            given[...] = low(total)

    @pl.when(which == 0)
    def _():
        write(rows, grads_pre)

    @pl.when(which == 1)
    def _():
        write(acts, grads_wide)


def pair_weight_grads(rows, grads_pre, acts, grads_wide):
    count, width = len(rows), rows[0].shape[1]
    tile = hidden_tile(width)
    tiles = width // tile
    last = tiles - 1

    def which(slot, fetched):
        return slot ^ fetched[0]

    def columns(arr, index):
        return pl.BlockSpec((arr.shape[0], tile), index)

    def row_index(slot, member, i, fetched):
        return (0, jnp.where(which(slot, fetched) == 0, i, 0))

    def pre_index(slot, member, i, fetched):
        return (0, jnp.where(which(slot, fetched) == 0, member, 0))

    def act_index(slot, member, i, fetched):
        return (0, jnp.where(which(slot, fetched) == 1, member * tiles + i, 0))

    def kept_index(slot, member, i, fetched):
        return (jnp.where(slot == 0, member, 1), jnp.where(slot == 0, i, last), 0)

    def given_index(slot, member, i, fetched):
        return (jnp.where(slot == 1, member, 0), jnp.where(slot == 1, i, 0), 0)

    depth = sum(arr.shape[0] for arr in rows)
    kept, given = pl.pallas_call(
        functools.partial(pair_weight_kernel, count),
        out_shape=[jax.ShapeDtypeStruct((2, width, width), jnp.bfloat16)] * 2,
        grid_spec=pltpu.PrefetchScalarGridSpec(
            num_scalar_prefetch=1,
            grid=(2, 2, tiles),
            in_specs=[columns(arr, row_index) for arr in rows]
            + [pl.BlockSpec((arr.shape[0], width), pre_index) for arr in grads_pre]
            + [columns(arr, act_index) for arr in acts]
            + [pl.BlockSpec(arr.shape, lambda s, m, i, f: (0, 0)) for arr in grads_wide],
            out_specs=[
                pl.BlockSpec((None, tile, width), kept_index),
                pl.BlockSpec((None, tile, width), given_index),
            ],
        ),
        compiler_params=pltpu.CompilerParams(vmem_limit_bytes=32 * 2**20),
        cost_estimate=pl.CostEstimate(
            flops=8 * depth * width * width,
            bytes_accessed=8 * width * width + 16 * depth * width,
            transcendentals=0,
        ),
    )(lax.axis_index("section").reshape(1), *rows, *grads_pre, *acts, *grads_wide)
    return low(kept.astype(jnp.float32) + section_swap(given).astype(jnp.float32))


def own_layer_kernel(fetched, zero_first, zero_second, one_first, one_second, moved, up, down):
    section = fetched[0]
    sums = ((zero_first, zero_second), (one_first, one_second))
    for layer in range(2):
        for k in range(2):

            @pl.when((section == layer) & (pl.program_id(0) == k))
            def _(layer=layer, k=k):
                mine, other = ((up, down), (down, up))[layer]
                mine[...] = sums[layer][k][...].astype(jnp.float32)
                other[...] = moved[...].astype(jnp.float32)


def own_layer_grads(zero_sums, one_sums):
    section = lax.axis_index("section")
    zero, one = [[arr[0] for arr in sums] for sums in (zero_sums, one_sums)]
    given = [jnp.where(section == 0, one[k], zero[k]) for k in range(2)]
    moved = section_swap(jnp.stack(given))
    height, width = zero[0].shape
    tile = height // 4

    def block_of(layer, number):
        def index(k, i, fetched):
            chosen = (fetched[0] == layer) & (k == number)
            return (jnp.where(chosen, i, 0), 0)

        return pl.BlockSpec((tile, width), index)

    stacked = pl.BlockSpec((None, tile, width), lambda k, i, fetched: (k, i, 0))
    return pl.pallas_call(
        own_layer_kernel,
        out_shape=[jax.ShapeDtypeStruct((2, height, width), jnp.float32)] * 2,
        grid_spec=pltpu.PrefetchScalarGridSpec(
            num_scalar_prefetch=1,
            grid=(2, height // tile),
            in_specs=[block_of(layer, k) for layer in range(2) for k in range(2)] + [stacked],
            out_specs=[stacked, stacked],
        ),
        compiler_params=pltpu.CompilerParams(vmem_limit_bytes=32 * 2**20),
    )(section.reshape(1), *zero, *one, moved)


def shards(
    tokens_in,
    cotangent,
    segments,
    routes,
    ln1_gain,
    w_qkv,
    w_out,
    ln2_gain,
    w_up,
    w_down,
    centroids,
    sub_gains,
    expert_up,
    expert_down,
):
    section = lax.axis_index("section")
    is_first = section == 0

    def mine(table):
        return lax.dynamic_index_in_dim(table, section, 0, keepdims=False)

    def theirs(table):
        return lax.dynamic_index_in_dim(table, 1 - section, 0, keepdims=False)

    def both_layers(own):
        other = section_swap(own)
        return (jnp.where(is_first, own, other), jnp.where(is_first, other, own))

    route_table = routes[0, :, :, 0]
    own_routes = mine(route_table)
    other_routes = section_swap(theirs(route_table))
    layer_routes = jnp.stack(
        [jnp.where(is_first, own_routes, other_routes), jnp.where(is_first, other_routes, own_routes)]
    )
    route_tables = wide_table(layer_routes)
    plane_rows = route_table.shape[1] * lax.axis_size("wide")
    orders = [token_order(plane_rows)] + [routed_order(route_tables[:, i]) for i in range(2)]
    changes = [order_change(orders[i], orders[i + 1]) for i in range(2)]

    def stacked_layers(own):
        return lax.all_gather(own, "section", axis=0, tiled=True)

    ln1_pair, ln2_pair = both_layers(ln1_gain[0]), both_layers(ln2_gain[0])
    qkv_pair, out_pair = both_layers(w_qkv[0]), both_layers(w_out[0])
    up_pair, down_pair = both_layers(w_up[0]), both_layers(w_down[0])
    center_pair, gain_pair = both_layers(centroids[0, 0]), both_layers(sub_gains[0, 0])
    def split_layer(layer):
        if layer == 0:
            piece = jnp.where(is_first, expert_ups, section_send(expert_downs, 0))
        else:
            piece = jnp.where(is_first, section_send(expert_ups, 1), expert_downs)
        return rep_pair_gather(piece[None])

    segment_ids = mine(segments)
    hidden = mine(tokens_in)
    expert_ups, expert_downs = after((expert_up[0, 0], expert_down[0, 0]), hidden)
    gathered = split_layer(0)
    layer_matrices = [None, None]
    second_inputs = (expert_ups, expert_downs)

    dense_weights = []
    for i in range(2):
        dense_weights.append(
            (
                ln1_pair[i],
                qkv_pair[i],
                out_pair[i],
                ln2_pair[i],
                [(up_pair[i], (), down_pair[i], ())],
            )
        )

    def expert_weights(layer):
        def sublayer_weights(k):
            mats = layer_matrices[layer]
            return [(mats, (0, i, k), mats, (1, i, k)) for i in range(2)]

        return (center_pair[layer], gain_pair[layer], sublayer_weights)

    slot_matrix = slot_matrix_of(layer_routes[1])
    grad = expert_trade(low(matmul_left(slot_matrix, mine(cotangent))))
    saved = []
    for layer in range(2):
        rows_in, dense_saved = dense_forward(
            hidden.astype(jnp.float32),
            segment_ids,
            dense_weights[layer],
            orders[layer],
            changes[layer],
        )
        layer_matrices[layer] = stacked_layers(after(gathered, dense_saved[-2][0])[None])
        if layer == 0:
            expert_ups, expert_downs = after(second_inputs, rows_in)
            gathered = split_layer(1)
        hidden, expert_saved = expert_forward(rows_in, *expert_weights(layer))
        saved.append((dense_saved, expert_saved))
    produced = low(matmul(slot_matrix, expert_trade(hidden)))

    grad, expert_one, parts, _ = expert_backward(low(grad), saved[1][1], *expert_weights(1), ())
    grad, dense_one, sums_one = dense_backward(
        grad, saved[1][0], segment_ids, dense_weights[1], orders[1], parts[1], parts[0], list
    )
    grad, expert_zero, parts, dense_one = expert_backward(
        low(grad), saved[0][1], *expert_weights(0), dense_one
    )
    grad, dense_zero, (expert_up_grad, expert_down_grad) = dense_backward(
        grad,
        saved[0][0],
        segment_ids,
        dense_weights[0],
        orders[0],
        parts[1],
        parts[0],
        lambda sums_zero: own_layer_grads(sums_zero, sums_one),
    )
    grads = [(dense_zero, expert_zero), (dense_one, expert_one)]

    half_width = produced.shape[1] // 2

    def halves_out(value):
        given = lax.dynamic_slice_in_dim(value, (1 - section) * half_width, half_width, 1)
        kept = lax.dynamic_slice_in_dim(value, section * half_width, half_width, 1)
        moved = section_swap(low(given)).astype(value.dtype)
        return jnp.stack([jnp.where(is_first, kept, moved), jnp.where(is_first, moved, kept)])

    block_out = halves_out(produced)
    grad_input = halves_out(grad)

    dense_pairs = list(zip(grads[0][0], grads[1][0]))
    gains_one, qkv_pair, out_pair, gains_two, up_pair, down_pair = dense_pairs
    gain_rows = jnp.stack([gains_one[0], gains_two[0], gains_one[1], gains_two[1]])
    gain_rows = gain_rows + section_swap(gain_rows)
    gain_rows = mine(gain_rows.reshape(2, 2, -1))
    gain_sums = small_scatter(small_scatter(gain_rows, "wide"), "rep")

    def own_sum(pair):
        first = pair[0].astype(jnp.float32) + section_send(low(pair[0]), 1).astype(jnp.float32)
        second = pair[1].astype(jnp.float32) + section_send(low(pair[1]), 0).astype(jnp.float32)
        return jnp.where(is_first, first, second)

    small = [jnp.concatenate([g[1][0][None]] + [v[None] for v in g[1][1]]) for g in grads]
    small_sum = small_scatter(own_sum(small), "rep")
    return (
        block_out,
        grad_input,
        gain_sums[0][None],
        both_halves(qkv_pair, 1)[None],
        both_halves(out_pair, 0)[None],
        gain_sums[1][None],
        both_halves(up_pair, 1)[None],
        both_halves(down_pair, 0)[None],
        small_sum[0][None, None],
        small_sum[1:][None, None],
        expert_up_grad[None, None],
        expert_down_grad[None, None],
    )


def solution(mesh):
    in_specs = (
        P(None, ("rep", "wide"), None),
        P(None, ("rep", "wide"), None),
        P(None, "rep"),
        P("section", None, ("rep", "wide"), None),
        P("section", None),
        P("section", None, "wide"),
        P("section", "wide", None),
        P("section", None),
        P("section", None, "wide"),
        P("section", "wide", None),
        P("section", "wide", None),
        P("section", "wide", None, None),
        P("section", "wide", None, None, "rep"),
        P("section", "wide", None, "rep", None),
    )
    out_specs = (
        P(None, ("rep", "wide"), "section"),
        P(None, ("rep", "wide"), "section"),
        P("section", ("wide", "rep")),
        P("section", "rep", "wide"),
        P("section", "wide", "rep"),
        P("section", ("wide", "rep")),
        P("section", "rep", "wide"),
        P("section", "wide", "rep"),
        P("section", "wide", "rep"),
        P("section", "wide", None, "rep"),
        P("section", "wide", None, None, "rep"),
        P("section", "wide", None, "rep", None),
    )
    return jax.shard_map(shards, mesh=mesh, in_specs=in_specs, out_specs=out_specs, check_vma=False)
```

```python
import functools
import math

import jax
import jax.numpy as jnp
from jax import lax
from jax.experimental import pallas as pl
from jax.experimental.pallas import tpu as pltpu
from jax.sharding import PartitionSpec as P

HD = 64
SEQ_LEN = 1024


epsilon = 1e-05
root_half = 1.0 / math.sqrt(2.0)
root_tau = 1.0 / math.sqrt(2.0 * math.pi)
masked_score = -1e30
highest_prec = lax.Precision.HIGHEST


def section_swap(value):
    return lax.ppermute(value, "section", [(0, 1), (1, 0)])


def section_send(value, source):
    return lax.ppermute(value, "section", [(source, 1 - source)])


def together(values):
    return lax.optimization_barrier(values)


def after(value, earlier):
    return lax.optimization_barrier((value, earlier))[0]


def unchanged(value):
    return value


def low(value):
    return value.astype(jnp.bfloat16)


def matmul(first_arg, second_arg):
    return jnp.dot(first_arg, second_arg, preferred_element_type=jnp.float32)


def matmul_left(first_arg, second_arg):
    return lax.dot_general(
        first_arg, second_arg, (((0,), (0,)), ((), ())), preferred_element_type=jnp.float32
    )


def matmul_right(first_arg, second_arg):
    return lax.dot_general(
        first_arg, second_arg, (((1,), (1,)), ((), ())), preferred_element_type=jnp.float32
    )


def hidden_tile(width):
    return min(512, width)


def row_steps(rows):
    step = min(256, rows)
    return [pl.ds(i, step) for i in range(0, rows, step)]


def store_parts(total, parts):
    size = parts[0].shape[0]
    for i, part in enumerate(parts):
        part[...] = total[pl.ds(i * size, size), :].astype(part.dtype)


def on_each_set(sets, steps, work):
    if len(sets) == 1:
        work(*sets[0])
        return
    for i, tiles in enumerate(sets):

        @pl.when(pl.program_id(0) // steps == i)
        def _(tiles=tiles):
            work(*tiles)


def mlp_forward_kernel(count, moves, sets, set_steps, *refs):
    blocks, refs = refs[:count], refs[count:]
    weights, refs = refs[: 2 * sets], refs[2 * sets :]
    weights = list(zip(weights[::2], weights[1::2]))
    if moves:
        moving, own_moving, middle, refs = refs[0], refs[1], refs[2], refs[3:]
    act, slope, rows_out = refs[:3]
    parts, total = refs[3:-1], refs[-1]
    step = pl.program_id(0)
    size = blocks[0].shape[0]
    steps = row_steps(total.shape[0])

    @pl.when(step == 0)
    def _():
        for i in range(count):
            rows_out[pl.ds(i * size, size), :] = blocks[i][...]
        if moves:
            for span in steps:
                total[span, :] = matmul(own_moving[span, :], middle[...])
        else:
            total[...] = jnp.zeros_like(total)

    def work(up_tile, down_tile):
        for span in steps:
            pre = matmul(rows_out[span, :], up_tile[...])
            below = 0.5 * (1.0 + lax.erf(pre * root_half))
            act[span, :] = low(pre * below)
            slope[span, :] = low(below + pre * (jnp.exp(-0.5 * pre * pre) * root_tau))
            if not moves:
                total[span, :] += matmul(act[span, :], down_tile[...])
        if moves:
            for span in steps:
                total[span, :] += matmul(low(matmul(moving[span, :], act[...])), down_tile[...])

    on_each_set(weights, set_steps, work)

    @pl.when(step == pl.num_programs(0) - 1)
    def _():
        store_parts(total, parts)


def mlp_backward_kernel(count, moves, sets, set_steps, *refs):
    blocks, slope, refs = refs[:count], refs[count], refs[count + 1 :]
    weights, refs = refs[: 2 * sets], refs[2 * sets :]
    weights = list(zip(weights[::2], weights[1::2]))
    if moves:
        moving, refs = refs[0], refs[1:]
    grad_pre, rows_out = refs[:2]
    parts, total = refs[2:-1], refs[-1]
    size = blocks[0].shape[0]
    steps = row_steps(total.shape[0])

    @pl.when(pl.program_id(0) == 0)
    def _():
        if moves:
            for span in steps:
                moved = jnp.zeros((span.size, total.shape[1]), jnp.float32)
                for i in range(count):
                    moved += matmul_left(moving[pl.ds(i * size, size), span], blocks[i][...])
                rows_out[span, :] = low(moved)
        else:
            for i in range(count):
                rows_out[pl.ds(i * size, size), :] = blocks[i][...]
        total[...] = jnp.zeros_like(total)

    def work(up_tile, down_tile):
        for span in steps:
            grad_act = matmul_right(rows_out[span, :], down_tile[...])
            grad_pre[span, :] = low(grad_act * slope[span, :].astype(jnp.float32))
            total[span, :] += matmul_right(grad_pre[span, :], up_tile[...])

    on_each_set(weights, set_steps, work)

    @pl.when(pl.program_id(0) == pl.num_programs(0) - 1)
    def _():
        store_parts(total, parts)


def in_hbm(arrays):
    return [pltpu.with_memory_space_constraint(arr, pltpu.HBM) for arr in arrays]


def mlp_call(kernel, blocks, streamed, resident, hidden_outs, weights):
    count, size = len(blocks), blocks[0].shape[0]
    rows, width = count * size, blocks[0].shape[1]
    set_width = weights[0][0].shape[-1]
    hidden = set_width * len(weights)
    tile = hidden_tile(set_width)
    set_steps = set_width // tile

    def whole(shape):
        return pl.BlockSpec(shape, lambda i: (0,) * len(shape))

    def tiles(lead, set_no, along_rows):
        def index(i):
            turn = jnp.clip(i - set_no * set_steps, 0, set_steps - 1)
            return lead + ((turn, 0) if along_rows else (0, turn))

        shape = (tile, width) if along_rows else (width, tile)
        return pl.BlockSpec((None,) * len(lead) + shape, index)

    columns = pl.BlockSpec((rows, tile), lambda i: (0, i))
    own_type = jnp.float32 if count > 1 else jnp.bfloat16
    part_types = [own_type] + [jnp.bfloat16] * (count - 1)
    weight_specs, matrices = ([], [])
    for set_no, (up_mat, up_lead, down_mat, down_lead) in enumerate(weights):
        weight_specs += [tiles(up_lead, set_no, False), tiles(down_lead, set_no, True)]
        matrices += [up_mat, down_mat]
    outs = pl.pallas_call(
        functools.partial(kernel, count, len(resident) > 0, len(weights), set_steps),
        grid=(hidden // tile,),
        in_specs=[whole(block.shape) for block in blocks]
        + [columns for _ in streamed]
        + weight_specs
        + [whole(arr.shape) for arr in resident],
        out_shape=[pltpu.HBM((rows, hidden), jnp.bfloat16)] * hidden_outs
        + [pltpu.HBM((rows, width), jnp.bfloat16)]
        + [jax.ShapeDtypeStruct((size, width), kind) for kind in part_types],
        out_specs=[columns] * hidden_outs
        + [whole((rows, width))]
        + [whole((size, width)) for _ in part_types],
        scratch_shapes=[pltpu.VMEM((rows, width), jnp.float32)],
        compiler_params=pltpu.CompilerParams(vmem_limit_bytes=40 * 2**20),
        cost_estimate=pl.CostEstimate(
            flops=4 * rows * width * hidden,
            bytes_accessed=4 * width * hidden + 6 * rows * width,
            transcendentals=2 * rows * hidden,
        ),
    )(*blocks, *in_hbm(streamed), *in_hbm(matrices), *in_hbm(resident))
    return outs[:hidden_outs], outs[hidden_outs], outs[hidden_outs + 1 :]


def mlp_forward(blocks, weights, moved=()):
    (act, slope), rows, parts = mlp_call(mlp_forward_kernel, blocks, (), moved, 2, weights)
    return (parts, (rows, act, slope))


def mlp_backward(blocks, slope, weights, moved=()):
    (grad_pre,), rows, parts = mlp_call(mlp_backward_kernel, blocks, (slope,), moved, 1, weights)
    return (parts, rows, grad_pre)


def norm_forward(values, gain_vec):
    center = values - jnp.mean(values, axis=-1, keepdims=True)
    scale_inv = lax.rsqrt(jnp.mean(center * center, axis=-1, keepdims=True) + epsilon)
    normal = center * scale_inv
    return (normal * gain_vec, normal, scale_inv)


def norm_backward(grad_out, normal, scale_inv, gain_vec):
    scaled = grad_out * gain_vec
    grad_values = scale_inv * (
        scaled
        - jnp.mean(scaled, axis=-1, keepdims=True)
        - normal * jnp.mean(scaled * normal, axis=-1, keepdims=True)
    )
    return (grad_values, jnp.sum(grad_out * normal, axis=0))


def is_square(axis):
    return lax.axis_size(axis) == 4


def wide_hop(value, mask):
    return lax.ppermute(value, "wide", [(i, i ^ mask) for i in range(4)])


def wide_spread(rows):
    if not is_square("wide"):
        return [lax.all_gather(rows, "wide", axis=0, tiled=True)]
    half = rows.shape[0] // 2
    y_first = wide_hop(rows[:half], 2)
    x_last = wide_hop(rows[half:], 1)
    y_last = wide_hop(rows[half:], 2)
    x_first = wide_hop(rows[:half], 1)
    d_first = wide_hop(y_first, 1)
    d_last = wide_hop(x_last, 2)
    return [
        rows,
        jnp.concatenate([x_first, x_last]),
        jnp.concatenate([y_first, y_last]),
        jnp.concatenate([d_first, d_last]),
    ]


def wide_collect(parts):
    if not is_square("wide"):
        return lax.psum_scatter(low(parts[0]), "wide", scatter_dimension=0, tiled=True).astype(
            jnp.float32
        )
    own = parts[0]
    x_part, y_part, d_low = [low(part) for part in parts[1:]]
    half = own.shape[0] // 2
    via_x = wide_hop(d_low[:half], 1)
    via_y = wide_hop(d_low[half:], 2)
    x_first = wide_hop(x_part[:half], 1)
    y_last = wide_hop(y_part[half:], 2)
    y_first = wide_hop(y_part[:half] + via_x, 2)
    x_last = wide_hop(x_part[half:] + via_y, 1)
    first = own[:half] + x_first.astype(jnp.float32) + y_first.astype(jnp.float32)
    last = own[half:] + x_last.astype(jnp.float32) + y_last.astype(jnp.float32)
    return jnp.concatenate([first, last])


def in_order(blocks):
    if len(blocks) == 1:
        return blocks[0]
    me = lax.axis_index("wide")
    stacked = jnp.stack(blocks)
    return jnp.concatenate(
        [lax.dynamic_index_in_dim(stacked, me ^ i, 0, keepdims=False) for i in range(4)]
    )


def in_blocks(values):
    if not is_square("wide"):
        return [values]
    me = lax.axis_index("wide")
    size = values.shape[0] // 4
    return [lax.dynamic_slice_in_dim(values, (me ^ i) * size, size, 0) for i in range(4)]


def expert_trade(values):
    return lax.all_to_all(values, "wide", split_axis=0, concat_axis=0, tiled=True)


def rep_hop(value, mask):
    return lax.ppermute(value, "rep", [(i, i ^ mask) for i in range(4)])


rep_pairs = [[0, 1], [2, 3]]


def rep_pair_gather(values):
    return lax.all_gather(values, "rep", axis=0, tiled=True, axis_index_groups=rep_pairs)


def rep_pair_scatter(values):
    return lax.psum_scatter(
        values, "rep", scatter_dimension=0, tiled=True, axis_index_groups=rep_pairs
    )


def rep_spread(rows):
    return [rows, rep_hop(rows, 2)]


def rep_collect(parts):
    return parts[0] + rep_hop(parts[1], 2).astype(jnp.float32)


def small_scatter(values, axis):
    if not is_square(axis):
        return lax.psum_scatter(values, axis, scatter_dimension=1, tiled=True)
    me = lax.axis_index(axis)
    size = values.shape[1] // 4

    def columns(device):
        return lax.dynamic_slice_in_dim(values, device * size, size, 1)

    total = columns(me)
    for mask in (1, 2, 3):
        pairs = [(i, i ^ mask) for i in range(4)]
        total = total + lax.ppermute(columns(me ^ mask), axis, pairs)
    return total


def joined(blocks):
    return blocks[0] if len(blocks) == 1 else jnp.concatenate(blocks)


def attention_layout(packed, segment_ids):
    row_count = packed.shape[0]
    head_count = packed.shape[1] // (3 * HD)
    seq_count = row_count // SEQ_LEN
    block_rows = min(512, SEQ_LEN)
    per_seq = SEQ_LEN // block_rows
    head_parts = packed.reshape(seq_count, SEQ_LEN, head_count, 3, HD)
    seg_table = segment_ids.reshape(seq_count, SEQ_LEN)
    return (head_parts, seg_table, block_rows, per_seq, head_count, seq_count)


def block_scores(seq_parts, seq_segs, row_start, block_rows):
    key_end = row_start + block_rows
    queries = seq_parts[row_start:key_end, :, 0]
    scores = jnp.einsum(
        "qhd,khd->hqk", queries, seq_parts[:key_end, :, 1], preferred_element_type=jnp.float32
    ) * (1.0 / math.sqrt(HD))
    seg_query = seq_segs[row_start:key_end]
    query_pos = row_start + jnp.arange(block_rows, dtype=jnp.int32)
    key_pos = jnp.arange(key_end, dtype=jnp.int32)
    allowed = (query_pos[:, None] >= key_pos[None, :]) & (
        seg_query[:, None] == seq_segs[None, :key_end]
    )
    return (jnp.where(allowed[None], scores, masked_score), queries)


def attention_forward(packed, segment_ids):
    head_parts, seg_table, block_rows, per_seq, head_count, seq_count = attention_layout(
        packed, segment_ids
    )

    def one_seq(seq_pack):
        seq_parts, seq_segs = seq_pack
        block_outs, block_logs = ([], [])
        for block_no in range(per_seq):
            row_start = block_no * block_rows
            key_end = row_start + block_rows
            scores, queries = block_scores(seq_parts, seq_segs, row_start, block_rows)
            highest = jnp.max(scores, axis=-1, keepdims=True)
            exponent = jnp.exp(scores - highest)
            row_total = jnp.sum(exponent, axis=-1, keepdims=True)
            probs_low = (exponent / row_total).astype(jnp.bfloat16)
            attended = jnp.einsum(
                "hqk,khd->qhd",
                probs_low,
                seq_parts[:key_end, :, 2],
                preferred_element_type=jnp.float32,
            )
            block_outs.append(attended.astype(jnp.bfloat16).reshape(block_rows, head_count * HD))
            block_logs.append(highest[..., 0] + jnp.log(row_total[..., 0]))
        return (jnp.concatenate(block_outs, axis=0), jnp.stack(block_logs))

    attended, log_totals = lax.map(one_seq, (head_parts, seg_table))
    return (attended.reshape(packed.shape[0], head_count * HD), log_totals)


def attention_backward(packed, segment_ids, log_totals, grad_att):
    head_parts, seg_table, block_rows, per_seq, head_count, seq_count = attention_layout(
        packed, segment_ids
    )
    grad_seqs = grad_att.reshape(seq_count, SEQ_LEN, head_count, HD)
    scale_value = 1.0 / math.sqrt(HD)

    def one_seq(seq_pack):
        seq_parts, seq_segs, seq_logs, seq_grad = seq_pack
        query_list = []
        grad_key = jnp.zeros((SEQ_LEN, head_count, HD), jnp.float32)
        grad_value = jnp.zeros((SEQ_LEN, head_count, HD), jnp.float32)
        for block_no in range(per_seq):
            row_start = block_no * block_rows
            key_end = row_start + block_rows
            scores, queries = block_scores(seq_parts, seq_segs, row_start, block_rows)
            probs = jnp.exp(scores - seq_logs[block_no][..., None])
            grad_here = seq_grad[row_start:key_end]
            grad_probs = jnp.einsum(
                "qhd,khd->hqk",
                grad_here,
                seq_parts[:key_end, :, 2],
                preferred_element_type=jnp.float32,
            )
            inner = jnp.sum(grad_probs * probs, axis=-1, keepdims=True)
            grad_scores = (probs * (grad_probs - inner)).astype(jnp.bfloat16)
            query_list.append(
                jnp.einsum(
                    "hqk,khd->qhd",
                    grad_scores,
                    seq_parts[:key_end, :, 1],
                    preferred_element_type=jnp.float32,
                )
                * scale_value
            )
            key_part = (
                jnp.einsum("hqk,qhd->khd", grad_scores, queries, preferred_element_type=jnp.float32)
                * scale_value
            )
            value_part = jnp.einsum(
                "hqk,qhd->khd",
                probs.astype(jnp.bfloat16),
                grad_here,
                preferred_element_type=jnp.float32,
            )
            pad_rows = ((0, SEQ_LEN - key_end), (0, 0), (0, 0))
            grad_key = grad_key + jnp.pad(key_part, pad_rows)
            grad_value = grad_value + jnp.pad(value_part, pad_rows)
        return (jnp.concatenate(query_list, axis=0), grad_key, grad_value)

    grad_query, grad_key, grad_value = lax.map(
        one_seq, (head_parts, seg_table, log_totals, grad_seqs)
    )
    stacked = jnp.stack([grad_query, grad_key, grad_value], axis=3)
    return stacked.reshape(packed.shape[0], head_count * 3 * HD).astype(jnp.bfloat16)


class RowOrder:
    def __init__(self, place):
        self.place = place
        self.count = place.shape[0]

    def onehot(self):
        rows = jnp.arange(self.count, dtype=jnp.int32)
        return (self.place[:, None] == rows[None, :]).astype(jnp.bfloat16)

    def to_tokens(self, rows):
        return low(matmul(self.onehot(), rows))

    def from_tokens(self, tokens):
        return low(matmul_left(self.onehot(), tokens))


def token_order(count):
    tokens = jnp.arange(count, dtype=jnp.int32)
    if not is_square("wide"):
        return RowOrder(tokens)
    return RowOrder(tokens ^ (lax.axis_index("wide") * (count // 4)))


def wide_table(values):
    if not is_square("wide"):
        return lax.all_gather(values, "wide", axis=0)
    me = lax.axis_index("wide")
    hops = jnp.stack([values] + [wide_hop(values, mask) for mask in (1, 2, 3)])
    return jnp.stack([lax.dynamic_index_in_dim(hops, me ^ i, 0, keepdims=False) for i in range(4)])


def routed_order(all_routes):
    devices, size = all_routes.shape
    experts = jnp.arange(devices, dtype=jnp.int32)
    tokens = jnp.arange(size, dtype=jnp.int32)
    same = (all_routes[:, :, None] == all_routes[:, None, :]) & (tokens[:, None] > tokens[None, :])
    rank_ids = jnp.sum(same.astype(jnp.int32), axis=2)
    owner = all_routes ^ lax.axis_index("wide") if is_square("wide") else all_routes
    place = owner * size + experts[:, None] * (size // devices) + rank_ids
    return RowOrder(place.reshape(-1))


def order_change(source, target):
    rows = jnp.arange(target.count, dtype=jnp.int32)
    found = (target.place[:, None] == rows[None, :]).astype(jnp.int32)
    return jnp.sum(found * source.place[:, None], axis=0)


def split(values):
    if not is_square("wide"):
        return [values]
    size = values.shape[0] // 4
    return [values[i * size : (i + 1) * size] for i in range(4)]


def own_start(size):
    return 0 if is_square("wide") else lax.axis_index("wide") * size


def dense_forward(block_in, segment_ids, weights, order, change_after, hooks):
    early_hook, middle_hook, late_hook = hooks
    first_norm_gain, qkv_mat, out_mat, second_norm_gain, mlp_weights = weights
    own_size = block_in.shape[0]
    shaped_one, normal_one, inv_one = norm_forward(block_in, first_norm_gain)
    first_blocks = wide_spread(early_hook(low(shaped_one)))
    packed = order.to_tokens(joined([low(matmul(rows, qkv_mat)) for rows in first_blocks]))
    attended, log_totals = attention_forward(packed, segment_ids)
    change = change_after(attended)
    attended = order.from_tokens(attended)
    middle = block_in + wide_collect([matmul(rows, out_mat) for rows in split(attended)])
    shaped_two, normal_two, inv_two = norm_forward(middle, second_norm_gain)
    second_blocks = middle_hook(wide_spread(low(shaped_two)))
    rows = jnp.arange(change.shape[0], dtype=jnp.int32)
    moving = (change[:, None] == rows[None, :]).astype(jnp.bfloat16)
    own_rows = own_start(own_size) + jnp.arange(own_size, dtype=jnp.int32)
    own_moving = (change[:, None] == own_rows[None, :]).astype(jnp.bfloat16)
    parts, mlp_saved = mlp_forward(second_blocks, mlp_weights, (moving, own_moving, low(middle)))
    parts = late_hook(parts)
    return (
        wide_collect(parts),
        (
            normal_one,
            inv_one,
            first_blocks,
            packed,
            attended,
            log_totals,
            normal_two,
            inv_two,
            mlp_saved,
            moving,
        ),
    )


def dense_backward(grad_rows, saved_state, segment_ids, weights, order, sums, last_part, finish):
    first_norm_gain, qkv_mat, out_mat, second_norm_gain, mlp_weights = weights
    (
        normal_one,
        inv_one,
        first_blocks,
        packed,
        attended,
        log_totals,
        normal_two,
        inv_two,
        (second_rows, activated, slope),
        moving,
    ) = saved_state
    own_size = grad_rows.shape[0]
    blocks, sums, last_part = together((wide_spread(grad_rows), sums, last_part))
    last_sum = rep_pair_scatter(last_part)
    parts, grad_wide, grad_pre = mlp_backward(blocks, slope, mlp_weights, (moving,))
    grad_out = lax.dynamic_slice_in_dim(grad_wide, own_start(own_size), own_size, 0)
    grad_norm_two = wide_collect(parts)
    down_part = half_given(weight_grad([activated], [grad_wide]), 0)
    up_part = half_given(weight_grad([second_rows], [grad_pre]), 1)
    grad_norm_two, down_part, up_part = together((grad_norm_two, down_part, up_part))
    grad_in_two, grad_gain_two = norm_backward(grad_norm_two, normal_two, inv_two, second_norm_gain)
    grad_middle = grad_out.astype(jnp.float32) + grad_in_two
    down_part, up_part = half_sum(down_part, 0), half_sum(up_part, 1)
    mid_blocks, last_sum, down_part, up_part = together(
        (wide_spread(low(grad_middle)), last_sum, down_part, up_part)
    )
    grad_down, grad_up = rep_summed(down_part, 1), rep_summed(up_part, 0)
    finished = finish([last_sum, sums])
    grad_att = order.to_tokens(joined([low(matmul_right(rows, out_mat)) for rows in mid_blocks]))
    grad_packed = attention_backward(packed, segment_ids, log_totals, grad_att)
    out_part = half_summed(weight_grad(row_blocks(attended, len(mid_blocks)), mid_blocks), 0)
    grad_packed, out_part = together((grad_packed, out_part))
    grad_packed = order.from_tokens(grad_packed)
    grad_norm_one = wide_collect([matmul_right(rows, qkv_mat) for rows in split(grad_packed)])
    qkv_part = half_summed(weight_grad(first_blocks, row_blocks(grad_packed, len(first_blocks))), 1)
    grad_out_mat = rep_summed(out_part, 1)
    grad_norm_one, qkv_part, finished, grad_down, grad_up = together(
        (grad_norm_one, qkv_part, finished, grad_down, grad_up)
    )
    grad_qkv = rep_summed(qkv_part, 0)
    grad_in_one, grad_gain_one = norm_backward(grad_norm_one, normal_one, inv_one, first_norm_gain)
    return (
        grad_middle + grad_in_one,
        (grad_gain_one, grad_qkv, grad_out_mat, grad_gain_two, grad_up, grad_down),
        finished,
    )


def half_given(partial, dim):
    size = partial.shape[dim] // 2
    other = (1 - lax.axis_index("section")) * size
    return partial, section_swap(lax.dynamic_slice_in_dim(partial, other, size, dim))


def half_sum(given, dim):
    partial, moved = given
    size = partial.shape[dim] // 2
    own = lax.axis_index("section") * size
    kept = lax.dynamic_slice_in_dim(partial, own, size, dim)
    return low(kept.astype(jnp.float32) + moved.astype(jnp.float32))


def half_summed(partial, dim):
    return half_sum(half_given(partial, dim), dim)


def rep_summed(partial, dim):
    return lax.psum_scatter(partial, "rep", scatter_dimension=dim, tiled=True)


def both_halves(layer_halves, dim):
    is_first = lax.axis_index("section") == 0
    first, second = layer_halves
    kept = jnp.where(is_first, first, second)
    moved = section_swap(jnp.where(is_first, second, first))
    parts = [jnp.where(is_first, kept, moved), jnp.where(is_first, moved, kept)]
    return jnp.concatenate(parts, axis=dim).astype(jnp.float32)


def slot_matrix_of(route_ids):
    expert_count = lax.axis_size("wide")
    capacity = max(2, route_ids.shape[0] // expert_count)
    onehot = (route_ids[:, None] == jnp.arange(expert_count, dtype=jnp.int32)[None, :]).astype(
        jnp.int32
    )
    rank_ids = jnp.sum(jnp.cumsum(onehot, axis=0) * onehot, axis=1) - 1
    position = route_ids * capacity + rank_ids
    return (
        position[:, None] == jnp.arange(expert_count * capacity, dtype=jnp.int32)[None, :]
    ).astype(jnp.bfloat16)


def weight_grad_kernel(count, *refs):
    rows, grads, out = refs[:count], refs[count:-1], refs[-1]
    total = matmul_left(rows[0][...], grads[0][...])
    for row, grad in zip(rows[1:], grads[1:]):
        total += matmul_left(row[...], grad[...])
    out[...] = low(total)


def row_blocks(values, count):
    return [(values, i, count) for i in range(count)]


def weight_grad(rows, grads):
    rows, grads = [
        [item if isinstance(item, tuple) else (item, 0, 1) for item in items] for items in (rows, grads)
    ]
    height, width = rows[0][0].shape[1], grads[0][0].shape[1]
    tile = hidden_tile(height)

    def block(item, columns, moving):
        arr, number, count = item
        return pl.BlockSpec(
            (arr.shape[0] // count, columns), lambda i: (number, i if moving else 0)
        )

    depth = sum(arr.shape[0] // count for arr, _, count in rows)
    return pl.pallas_call(
        functools.partial(weight_grad_kernel, len(rows)),
        grid=(height // tile,),
        in_specs=[block(item, tile, True) for item in rows]
        + [block(item, width, False) for item in grads],
        out_shape=jax.ShapeDtypeStruct((height, width), jnp.bfloat16),
        out_specs=pl.BlockSpec((tile, width), lambda i: (i, 0)),
        compiler_params=pltpu.CompilerParams(vmem_limit_bytes=24 * 2**20),
        cost_estimate=pl.CostEstimate(
            flops=2 * depth * height * width,
            bytes_accessed=2 * (depth * (height + width) + height * width),
            transcendentals=0,
        ),
    )(*[item[0] for item in rows], *[item[0] for item in grads])


def chunked(values):
    half = values.shape[0] // 2
    return [values[:half], values[half:]]


def expert_forward(rows_in, centroid, gain_rows, mlp_weights):
    hidden, saved = ([], [])
    starts = [low(rows) for rows in chunked(rows_in)]
    states = [rows.astype(jnp.float32) for rows in starts]
    sublayer_saved = []
    for sublayer in range(2):
        kept = []
        for i, current in enumerate(states):
            shaped, normal, scale_inv = norm_forward(current, gain_rows[sublayer])
            shaped = low(shaped)
            blocks = rep_spread(shaped)
            parts, mlp_saved = mlp_forward(blocks, mlp_weights(sublayer))
            kept.append((normal, scale_inv, mlp_saved))
            states[i] = current + rep_collect(parts)
        sublayer_saved.append(kept)
    for arrived, current in zip(starts, states):
        starting_rows = arrived.astype(jnp.float32)
        gate_value = jax.nn.sigmoid(jnp.dot(arrived, centroid, preferred_element_type=jnp.float32))
        gate = gate_value[:, None]
        hidden.append(low(gate * current + (1.0 - gate) * starting_rows))
        saved.append((arrived, gate_value, current))
    return (jnp.concatenate(hidden), (saved, sublayer_saved))


def expert_backward(grad_rows, saved_state, centroid, gain_rows, mlp_weights, mid):
    saved, sublayer_saved = saved_state
    states, start_grads = ([], [])
    grad_centroid = jnp.zeros(centroid.shape, jnp.float32)
    for rows, (arrived, gate_value, final_state) in zip(chunked(grad_rows), saved):
        starting_rows = arrived.astype(jnp.float32)
        grad_mixed = rows.astype(jnp.float32)
        grad_gate = jnp.sum(grad_mixed * (final_state - starting_rows), axis=-1)
        grad_logit = grad_gate * gate_value * (1.0 - gate_value)
        grad_centroid += jnp.dot(grad_logit, starting_rows, precision=highest_prec)
        states.append(gate_value[:, None] * grad_mixed)
        start_grads.append(
            (1.0 - gate_value[:, None]) * grad_mixed
            + grad_logit[:, None] * centroid.astype(jnp.float32)[None, :]
        )
    gain_list, weight_grads = ([], [])
    for sublayer in (1, 0):
        collected, pieces = ([], [])
        for i, (_, _, (rows, act, slope)) in enumerate(sublayer_saved[sublayer]):
            given = low(states[i])
            blocks = rep_spread(given)
            parts, grad_wide, grad_pre = mlp_backward(blocks, slope, mlp_weights(sublayer))
            collected.append(rep_collect(parts))
            pieces.append((act, grad_wide, rows, grad_pre))
        if sublayer == 0:
            collected[0], weight_grads, mid = together((collected[0], weight_grads, mid))
            weight_grads = [rep_pair_scatter(part) for part in weight_grads]
        acts, grads_wide, rows, grads_pre = zip(*pieces)
        weight_grads.append(pair_weight_grads(rows, grads_pre, acts, grads_wide))
        gain = 0.0
        for i, (normal, scale_inv, _) in enumerate(sublayer_saved[sublayer]):
            grad_values, grad_gain = norm_backward(
                collected[i], normal, scale_inv, gain_rows[sublayer]
            )
            gain += grad_gain
            states[i] = states[i] + grad_values
        gain_list.append(gain)
    grad_start = jnp.concatenate([low(a + b) for a, b in zip(start_grads, states)])
    return (grad_start, (grad_centroid, gain_list[::-1]), weight_grads[::-1], mid)


def pair_weight_kernel(count, prefetched, *refs):
    rows, grads_pre, acts, grads_wide = [refs[i * count : (i + 1) * count] for i in range(4)]
    kept, given = refs[4 * count :]
    which = pl.program_id(0) ^ prefetched[0]

    def write(lefts, rights):
        total = matmul_left(lefts[0][...], rights[0][...])
        for left, right in zip(lefts[1:], rights[1:]):
            total += matmul_left(left[...], right[...])

        @pl.when(pl.program_id(0) == 0)
        def _():
            kept[...] = low(total)

        @pl.when(pl.program_id(0) == 1)
        def _():
            given[...] = low(total)

    @pl.when(which == 0)
    def _():
        write(rows, grads_pre)

    @pl.when(which == 1)
    def _():
        write(acts, grads_wide)


def pair_weight_grads(rows, grads_pre, acts, grads_wide):
    count, width = len(rows), rows[0].shape[1]
    tile = hidden_tile(width)
    tiles = width // tile
    last = tiles - 1

    def which(slot, fetched):
        return slot ^ fetched[0]

    def columns(arr, index):
        return pl.BlockSpec((arr.shape[0], tile), index)

    def row_index(slot, member, i, fetched):
        return (0, jnp.where(which(slot, fetched) == 0, i, 0))

    def pre_index(slot, member, i, fetched):
        return (0, jnp.where(which(slot, fetched) == 0, member, 0))

    def act_index(slot, member, i, fetched):
        return (0, jnp.where(which(slot, fetched) == 1, member * tiles + i, 0))

    def kept_index(slot, member, i, fetched):
        return (jnp.where(slot == 0, member, 1), jnp.where(slot == 0, i, last), 0)

    def given_index(slot, member, i, fetched):
        return (jnp.where(slot == 1, member, 0), jnp.where(slot == 1, i, 0), 0)

    depth = sum(arr.shape[0] for arr in rows)
    kept, given = pl.pallas_call(
        functools.partial(pair_weight_kernel, count),
        out_shape=[jax.ShapeDtypeStruct((2, width, width), jnp.bfloat16)] * 2,
        grid_spec=pltpu.PrefetchScalarGridSpec(
            num_scalar_prefetch=1,
            grid=(2, 2, tiles),
            in_specs=[columns(arr, row_index) for arr in rows]
            + [pl.BlockSpec((arr.shape[0], width), pre_index) for arr in grads_pre]
            + [columns(arr, act_index) for arr in acts]
            + [pl.BlockSpec(arr.shape, lambda s, m, i, f: (0, 0)) for arr in grads_wide],
            out_specs=[
                pl.BlockSpec((None, tile, width), kept_index),
                pl.BlockSpec((None, tile, width), given_index),
            ],
        ),
        compiler_params=pltpu.CompilerParams(vmem_limit_bytes=32 * 2**20),
        cost_estimate=pl.CostEstimate(
            flops=8 * depth * width * width,
            bytes_accessed=8 * width * width + 16 * depth * width,
            transcendentals=0,
        ),
    )(
        lax.axis_index("section").reshape(1),
        *in_hbm(rows),
        *in_hbm(grads_pre),
        *in_hbm(acts),
        *in_hbm(grads_wide),
    )
    return low(kept.astype(jnp.float32) + section_swap(given).astype(jnp.float32))


def own_layer_kernel(fetched, zero_first, zero_second, one_first, one_second, moved, up, down):
    section = fetched[0]
    sums = ((zero_first, zero_second), (one_first, one_second))
    for layer in range(2):
        for k in range(2):

            @pl.when((section == layer) & (pl.program_id(0) == k))
            def _(layer=layer, k=k):
                mine, other = ((up, down), (down, up))[layer]
                mine[...] = sums[layer][k][...].astype(jnp.float32)
                other[...] = moved[...].astype(jnp.float32)


def own_layer_grads(zero_sums, one_sums):
    section = lax.axis_index("section")
    zero, one = [[arr[0] for arr in sums] for sums in (zero_sums, one_sums)]
    given = [jnp.where(section == 0, one[k], zero[k]) for k in range(2)]
    moved = section_swap(jnp.stack(given))
    height, width = zero[0].shape
    tile = height // 4

    def block_of(layer, number):
        def index(k, i, fetched):
            chosen = (fetched[0] == layer) & (k == number)
            return (jnp.where(chosen, i, 0), 0)

        return pl.BlockSpec((tile, width), index)

    stacked = pl.BlockSpec((None, tile, width), lambda k, i, fetched: (k, i, 0))
    return pl.pallas_call(
        own_layer_kernel,
        out_shape=[jax.ShapeDtypeStruct((2, height, width), jnp.float32)] * 2,
        grid_spec=pltpu.PrefetchScalarGridSpec(
            num_scalar_prefetch=1,
            grid=(2, height // tile),
            in_specs=[block_of(layer, k) for layer in range(2) for k in range(2)] + [stacked],
            out_specs=[stacked, stacked],
        ),
        compiler_params=pltpu.CompilerParams(vmem_limit_bytes=32 * 2**20),
    )(section.reshape(1), *zero, *one, moved)


def shards(
    tokens_in,
    cotangent,
    segments,
    routes,
    ln1_gain,
    w_qkv,
    w_out,
    ln2_gain,
    w_up,
    w_down,
    centroids,
    sub_gains,
    expert_up,
    expert_down,
):
    section = lax.axis_index("section")
    is_first = section == 0

    def mine(table):
        return lax.dynamic_index_in_dim(table, section, 0, keepdims=False)

    def theirs(table):
        return lax.dynamic_index_in_dim(table, 1 - section, 0, keepdims=False)

    def both_layers(own):
        other = section_swap(own)
        return (jnp.where(is_first, own, other), jnp.where(is_first, other, own))

    route_table = routes[0, :, :, 0]
    own_routes = mine(route_table)
    other_routes = section_swap(theirs(route_table))
    layer_routes = jnp.stack(
        [jnp.where(is_first, own_routes, other_routes), jnp.where(is_first, other_routes, own_routes)]
    )
    route_tables = wide_table(layer_routes)
    orders = [token_order(route_table.shape[1] * lax.axis_size("wide")), None, None]

    def change_after(layer):
        def change(event):
            orders[layer + 1] = routed_order(after(route_tables[:, layer], event))
            return order_change(orders[layer], orders[layer + 1])

        return change

    def stacked_layers(own):
        return lax.all_gather(own, "section", axis=0, tiled=True)

    ln1_pair, ln2_pair = both_layers(ln1_gain[0]), both_layers(ln2_gain[0])
    qkv_pair, out_pair = both_layers(w_qkv[0]), both_layers(w_out[0])
    up_pair, down_pair = both_layers(w_up[0]), both_layers(w_down[0])
    center_pair, gain_pair = both_layers(centroids[0, 0]), both_layers(sub_gains[0, 0])
    def split_layer(layer):
        if layer == 0:
            piece = jnp.where(is_first, expert_ups, section_send(expert_downs, 0))
        else:
            piece = jnp.where(is_first, section_send(expert_ups, 1), expert_downs)
        return piece[None]

    segment_ids = mine(segments)
    hidden = mine(tokens_in)
    expert_ups, expert_downs = after((expert_up[0, 0], expert_down[0, 0]), hidden)
    layer_matrices = [None, None]
    second_inputs = (expert_ups, expert_downs)

    dense_weights = []
    for i in range(2):
        dense_weights.append(
            (
                ln1_pair[i],
                qkv_pair[i],
                out_pair[i],
                ln2_pair[i],
                [(up_pair[i], (), down_pair[i], ())],
            )
        )

    def expert_weights(layer):
        def sublayer_weights(k):
            mats = layer_matrices[layer]
            return [(mats, (0, i, k), mats, (1, i, k)) for i in range(2)]

        return (center_pair[layer], gain_pair[layer], sublayer_weights)

    slot_matrix = slot_matrix_of(layer_routes[1])
    grad = expert_trade(low(matmul_left(slot_matrix, mine(cotangent))))
    saved = []
    for layer in range(2):
        gathering = []

        def early(value):
            value, piece = together((value, split_layer(0)))
            gathering.append(rep_pair_gather(piece))
            return value

        def later(value):
            value, own_gathered = together((value, gathering[0] if layer == 0 else gathered))
            gathering.append(own_gathered)
            return value

        rows_in, dense_saved = dense_forward(
            hidden.astype(jnp.float32),
            segment_ids,
            dense_weights[layer],
            orders[layer],
            change_after(layer),
            (early, unchanged, later) if layer == 0 else (unchanged, later, unchanged),
        )
        layer_matrices[layer] = stacked_layers(gathering[-1][None])
        if layer == 0:
            expert_ups, expert_downs = after(second_inputs, rows_in)
            gathered = rep_pair_gather(split_layer(1))
        hidden, expert_saved = expert_forward(rows_in, *expert_weights(layer))
        saved.append((dense_saved, expert_saved))
    produced = low(matmul(slot_matrix, expert_trade(hidden)))

    grad, expert_one, parts, _ = expert_backward(low(grad), saved[1][1], *expert_weights(1), ())
    grad, dense_one, sums_one = dense_backward(
        grad, saved[1][0], segment_ids, dense_weights[1], orders[1], parts[1], parts[0], list
    )
    grad, expert_zero, parts, dense_one = expert_backward(
        low(grad), saved[0][1], *expert_weights(0), dense_one
    )
    grad, dense_zero, (expert_up_grad, expert_down_grad) = dense_backward(
        grad,
        saved[0][0],
        segment_ids,
        dense_weights[0],
        orders[0],
        parts[1],
        parts[0],
        lambda sums_zero: own_layer_grads(sums_zero, sums_one),
    )
    grads = [(dense_zero, expert_zero), (dense_one, expert_one)]

    half_width = produced.shape[1] // 2

    def halves_out(value):
        given = lax.dynamic_slice_in_dim(value, (1 - section) * half_width, half_width, 1)
        kept = lax.dynamic_slice_in_dim(value, section * half_width, half_width, 1)
        moved = section_swap(low(given)).astype(value.dtype)
        return jnp.stack([jnp.where(is_first, kept, moved), jnp.where(is_first, moved, kept)])

    block_out = halves_out(produced)
    grad_input = halves_out(grad)

    dense_pairs = list(zip(grads[0][0], grads[1][0]))
    gains_one, qkv_pair, out_pair, gains_two, up_pair, down_pair = dense_pairs
    gain_rows = jnp.stack([gains_one[0], gains_two[0], gains_one[1], gains_two[1]])
    gain_rows = gain_rows + section_swap(gain_rows)
    gain_rows = mine(gain_rows.reshape(2, 2, -1))
    gain_sums = small_scatter(small_scatter(gain_rows, "wide"), "rep")

    def own_sum(pair):
        first = pair[0].astype(jnp.float32) + section_send(low(pair[0]), 1).astype(jnp.float32)
        second = pair[1].astype(jnp.float32) + section_send(low(pair[1]), 0).astype(jnp.float32)
        return jnp.where(is_first, first, second)

    small = [jnp.concatenate([g[1][0][None]] + [v[None] for v in g[1][1]]) for g in grads]
    small_sum = small_scatter(own_sum(small), "rep")
    return (
        block_out,
        grad_input,
        gain_sums[0][None],
        both_halves(qkv_pair, 1)[None],
        both_halves(out_pair, 0)[None],
        gain_sums[1][None],
        both_halves(up_pair, 1)[None],
        both_halves(down_pair, 0)[None],
        small_sum[0][None, None],
        small_sum[1:][None, None],
        expert_up_grad[None, None],
        expert_down_grad[None, None],
    )


def solution(mesh):
    in_specs = (
        P(None, ("rep", "wide"), None),
        P(None, ("rep", "wide"), None),
        P(None, "rep"),
        P("section", None, ("rep", "wide"), None),
        P("section", None),
        P("section", None, "wide"),
        P("section", "wide", None),
        P("section", None),
        P("section", None, "wide"),
        P("section", "wide", None),
        P("section", "wide", None),
        P("section", "wide", None, None),
        P("section", "wide", None, None, "rep"),
        P("section", "wide", None, "rep", None),
    )
    out_specs = (
        P(None, ("rep", "wide"), "section"),
        P(None, ("rep", "wide"), "section"),
        P("section", ("wide", "rep")),
        P("section", "rep", "wide"),
        P("section", "wide", "rep"),
        P("section", ("wide", "rep")),
        P("section", "rep", "wide"),
        P("section", "wide", "rep"),
        P("section", "wide", "rep"),
        P("section", "wide", None, "rep"),
        P("section", "wide", None, None, "rep"),
        P("section", "wide", None, "rep", None),
    )
    return jax.shard_map(shards, mesh=mesh, in_specs=in_specs, out_specs=out_specs, check_vma=False)
```
